128 devices in a mesh: chan: 8 (over z, core), tile: 16 (over x, y).
Axes of the slice: x: 4, y: 4, z: 4, core: 2. Of those that a mesh axis runs over, the one named last changes fastest.
Arguments:
- voltages: bfloat16 [2, 1024, 65536], P(None, 'tile', 'chan'), may hold values from -20 to 20
- flags: int32 [1024], replicated, may hold values 0 or 1
Outputs:
- visibilities: bfloat16 [2, 256, 1024, 1024], P(None, 'chan', 'tile')
- gains: float32 [2, 256, 1024], P(None, 'chan', 'tile')
The draws below stay inside these ranges and needn't reach their ends.
All inputs are finite; a program needn't handle non-finite values.
Results may differ from the reference program's by a relative error of at most 0.0069.
Values may be sent and summed in bfloat16 or wider, within the bound.
No kernel may reach another device: no remote copies, remote signals or barrier semaphores. Data moves between devices by JAX's collectives and lax.ppermute only.
A program may use at most 192 MiB of HBM per device.

```python
import math
import jax
import jax.numpy as jnp
from jax import lax

INPUTS = 1024
NCH = 256
TAPS = 16
ITERS = 3
NSPEC = 256


def draw_voltages(key, part):
    key = jax.random.fold_in(key, 11)
    keys = jax.random.split(key, 5)
    length = NSPEC * NCH
    signal = jnp.clip(jax.random.normal(keys[0], (2, length), jnp.float32), -5.0, 5.0)
    magnitude = jnp.exp(jax.random.uniform(keys[1], (INPUTS,), jnp.float32, jnp.log(0.5), jnp.log(2.0)))
    phase = jax.random.uniform(keys[2], (INPUTS,), jnp.float32, -1.0, 1.0)
    amplitude = 0.12
    noise = jnp.clip(jax.random.normal(keys[3], (2, INPUTS, length), jnp.float32), -5.0, 5.0)
    spread = jnp.exp(jax.random.uniform(keys[4], (INPUTS,), jnp.float32, jnp.log(0.6), jnp.log(1.6)))
    real_gain = (amplitude * magnitude * jnp.cos(phase))[:, None]
    imag_gain = (amplitude * magnitude * jnp.sin(phase))[:, None]
    real_part = real_gain * signal[0][None, :] - imag_gain * signal[1][None, :] + spread[:, None] * noise[0]
    imag_part = real_gain * signal[1][None, :] + imag_gain * signal[0][None, :] + spread[:, None] * noise[1]
    return jnp.stack([real_part, imag_part]).astype(jnp.bfloat16)


def plant(entries, stream_key, low, largest):
    extent = entries.shape
    index_at = [jax.random.randint(jax.random.fold_in(stream_key, axis), (), 0, extent[axis]) for axis in range(len(extent))]
    entries = entries.at[tuple(index_at)].set(low)
    longest = extent.index(max(extent))
    index_at[longest] = (index_at[longest] + 1) % extent[longest]
    return entries.at[tuple(index_at)].set(largest)


def setup_inputs(seed: int = 0) -> dict:
    seeds = jax.random.split(jax.random.key(seed), 3)
    voltages = draw_voltages(jax.random.fold_in(seeds[2], 71), 0)
    flags = plant((jax.random.randint(seeds[1], (INPUTS,), 0, 8) < 1).astype(jnp.int32), jax.random.fold_in(seeds[1], 1), 0, 1)
    return dict(voltages=voltages, flags=flags)


def taps_table(taps, channels):
    length = taps * channels
    index = jnp.arange(length, dtype=jnp.float32)
    centre = (length - 1) / 2.0
    shaped = jnp.sinc((index - centre) / channels)
    window = 0.5 - 0.5 * jnp.cos(2.0 * math.pi * (index + 0.5) / length)
    values = shaped * window
    values = values * jnp.sqrt(channels / jnp.sum(values * values))
    return values.reshape(taps, channels)

def dft_table(channels):
    index = jnp.arange(channels, dtype=jnp.int32)
    product = index[:, None] * index[None, :] % channels
    angle = 2.0 * math.pi / channels * product.astype(jnp.float32)
    scale = 1.0 / math.sqrt(channels)
    cosine = jnp.cos(angle) * scale
    sine = jnp.sin(angle) * scale
    upper = jnp.stack([cosine, -sine], axis=1)
    lower = jnp.stack([sine, cosine], axis=1)
    return jnp.concatenate([upper, lower], axis=0).astype(jnp.bfloat16)

def matvec(matrix, vector):
    return jnp.dot(matrix, vector, precision=lax.Precision.HIGHEST, preferred_element_type=jnp.float32)

def reference(voltages, flags):
    frames = voltages.reshape(2, INPUTS, NSPEC, NCH)
    padded = jnp.pad(frames, ((0, 0), (0, 0), (TAPS - 1, 0), (0, 0)))
    coefficients = taps_table(TAPS, NCH)
    filtered = coefficients[0] * padded[:, :, 0:NSPEC, :].astype(jnp.float32)
    for step in range(1, TAPS):
        filtered = filtered + coefficients[step] * padded[:, :, step:step + NSPEC, :].astype(jnp.float32)
    filtered = filtered.astype(jnp.bfloat16)
    joined = jnp.concatenate([filtered[0], filtered[1]], axis=-1)
    spectra = jnp.einsum('imj,jrk->krim', joined.astype(jnp.float32), dft_table(NCH).astype(jnp.float32), precision=lax.Precision.HIGHEST).astype(jnp.bfloat16)
    keep = (1 - flags).astype(jnp.float32)
    inverse = 1.0 / NSPEC

    def channel(block):
        signal = block.astype(jnp.float32)
        first = signal[0]
        second = signal[1]
        real_sum = (jnp.dot(first, first.T, precision=lax.Precision.HIGHEST, preferred_element_type=jnp.float32) + jnp.dot(second, second.T, precision=lax.Precision.HIGHEST, preferred_element_type=jnp.float32)) * inverse
        imag_sum = (jnp.dot(second, first.T, precision=lax.Precision.HIGHEST, preferred_element_type=jnp.float32) - jnp.dot(first, second.T, precision=lax.Precision.HIGHEST, preferred_element_type=jnp.float32)) * inverse
        diag_real = jnp.diagonal(real_sum)
        diag_imag = jnp.diagonal(imag_sum)
        current = jnp.stack([keep, jnp.zeros_like(keep)])
        for step in range(ITERS):
            total = jnp.sum(current * current)
            num_real = matvec(real_sum, current[0]) - matvec(imag_sum, current[1]) - (diag_real * current[0] - diag_imag * current[1])
            num_imag = matvec(real_sum, current[1]) + matvec(imag_sum, current[0]) - (diag_real * current[1] + diag_imag * current[0])
            denominator = total - (current[0] * current[0] + current[1] * current[1])
            updated = jnp.stack([num_real, num_imag]) * keep / denominator
            if step % 2 == 1:
                updated = 0.5 * (updated + current)
            current = updated
        return (jnp.stack([real_sum, imag_sum]).astype(jnp.bfloat16), current)
    visibilities, gains = lax.map(channel, spectra)
    return (jnp.transpose(visibilities, (1, 0, 2, 3)), jnp.transpose(gains, (1, 0, 2)))
```

```python
import functools
import math

import jax
import jax.numpy as jnp
import numpy as np
from jax import lax
from jax.experimental import pallas as pl
from jax.experimental.pallas import tpu as pltpu
from jax.sharding import PartitionSpec as P

NCH = 256
TAPS = 16
ITERS = 3
VMEM = 56 * 1024 * 1024


def taps_table():
    length = TAPS * NCH
    index = np.arange(length, dtype=np.float64)
    centre = (length - 1) / 2.0
    window = 0.5 - 0.5 * np.cos(2.0 * math.pi * (index + 0.5) / length)
    values = np.sinc((index - centre) / NCH) * window
    values = values * np.sqrt(NCH / np.sum(values * values))
    return values.reshape(TAPS, NCH).astype(np.float32)


def dft_table():
    index = np.arange(NCH)
    angle = (2.0 * math.pi / NCH) * (index[:, None] * index[None, :] % NCH)
    scale = 1.0 / math.sqrt(NCH)
    cosine = np.cos(angle) * scale
    sine = np.sin(angle) * scale
    real = np.concatenate([cosine, sine], axis=1)
    imag = np.concatenate([-sine, cosine], axis=1)
    return np.stack([real, imag], axis=1).reshape(2 * NCH, 2 * NCH).astype(np.float32)


def spectra_kernel(v_ref, h_ref, taps_ref, table_ref, out_ref, x_ref, wide_ref):
    history = TAPS - 1
    frames = v_ref.shape[2] // NCH

    def filter_tile(index, _):
        part = index // 8
        rows = pl.multiple_of((index // 2) % 4 * 16, 16)
        lane = pl.multiple_of(index % 2 * 128, 128)
        taps = [taps_ref[pl.ds(t, 1), pl.ds(lane, 128)] for t in range(TAPS)]
        window = []
        for f in range(history + frames):
            if f < history:
                tile = h_ref[part, pl.ds(rows, 16), pl.ds(lane + f * NCH, 128)]
            else:
                tile = v_ref[part, pl.ds(rows, 16), pl.ds(lane + (f - history) * NCH, 128)]
            window.append(tile.astype(jnp.float32))
            if f < history:
                continue
            m = f - history
            total = taps[0] * window[m]
            for t in range(1, TAPS):
                total = total + taps[t] * window[m + t]
            x_ref[pl.ds(rows + m * 64, 16), pl.ds(part * NCH + lane, 128)] = total.astype(jnp.bfloat16)
        return 0

    lax.fori_loop(0, 16, filter_tile, 0)

    pairs = frames // 2
    for block in range(pairs // 2):
        spectra = lax.dot_general(
            table_ref[...],
            x_ref[pl.ds(block * 256, 256), :],
            (((1,), (1,)), ((), ())),
            preferred_element_type=jnp.float32,
        )
        for half in range(2):
            wide_ref[pl.ds(block * 2 + half, 2 * NCH, stride=pairs), :] = spectra[:, half * 128 : half * 128 + 128]

    def narrow(index, _):
        rows = pl.multiple_of(index * 64, 64)
        tile = wide_ref[pl.ds(pl.multiple_of(index * 64 * pairs, 64), 64 * pairs), :]
        out_ref[pl.ds(rows, 64)] = tile.astype(jnp.bfloat16).reshape(64, pairs, 128)
        return 0

    lax.fori_loop(0, 2 * NCH // 64, narrow, 0)


def real_kernel(recv_ref, series_ref, across_ref, vis_ref):
    @pl.when(pl.program_id(1) == 0)
    def _():
        times = recv_ref.shape[0] * recv_ref.shape[4]
        for part in range(2):
            for pair in range(8):
                first = recv_ref[:, 2 * pair, 0, part].reshape(times, 128)
                second = recv_ref[:, 2 * pair + 1, 0, part].reshape(times, 128)
                low = jnp.concatenate([first[:, :64], second[:, :64]], axis=1)
                high = jnp.concatenate([first[:, 64:], second[:, 64:]], axis=1)
                start = part * 2 * times
                lanes = slice(pair * 128, pair * 128 + 128)
                series_ref[0, start : start + times, lanes] = low
                series_ref[0, start + times : start + 2 * times, lanes] = high
                across_ref[0, lanes, start : start + times] = low.T
                across_ref[0, lanes, start + times : start + 2 * times] = high.T

    tiles, _, rows, inputs = vis_ref.shape
    count = tiles * rows
    left = across_ref[0, pl.ds(pl.multiple_of(pl.program_id(1) * count, count), count), :]
    sums = jnp.dot(left, series_ref[0], preferred_element_type=jnp.float32)
    sums = sums * (2.0 / series_ref.shape[1])
    vis_ref[:, 0] = sums.astype(jnp.bfloat16).reshape(tiles, rows, inputs)


def imag_kernel(series_ref, across_ref, vis_ref):
    tiles, _, rows, inputs = vis_ref.shape
    half = series_ref.shape[1] // 2
    left = jnp.concatenate([across_ref[0, :, half:], -across_ref[0, :, :half]], axis=1)
    sums = jnp.dot(left, series_ref[0], preferred_element_type=jnp.float32)
    sums = sums * (1.0 / half)
    vis_ref[:, 0] = sums.astype(jnp.bfloat16).reshape(tiles, rows, inputs)


def gains_kernel(series_ref, flags_ref, out_ref):
    half = series_ref.shape[1] // 2
    step_rows = 32
    steps = half // step_rows
    inverse = 1.0 / half
    keep = (1 - flags_ref[...]).astype(jnp.float32)

    def load(step):
        start = pl.multiple_of(step * step_rows, step_rows)
        real = series_ref[0, pl.ds(start, step_rows), :].astype(jnp.float32)
        imag = series_ref[0, pl.ds(half + start, step_rows), :].astype(jnp.float32)
        return real, imag

    def fold(value):
        total = value[0:8]
        for row in range(8, step_rows, 8):
            total = total + value[row : row + 8]
        return total

    zeros = jnp.zeros((8, keep.shape[1]), jnp.float32)

    def diagonal_step(step, carry):
        real, imag = load(step)
        return (
            carry[0] + fold(real * real + imag * imag),
            carry[1] + fold(imag * real - real * imag),
        )

    diag = lax.fori_loop(0, steps, diagonal_step, (zeros, zeros))
    diag_real = jnp.sum(diag[0], axis=0, keepdims=True) * inverse
    diag_imag = jnp.sum(diag[1], axis=0, keepdims=True) * inverse

    gain_real = keep
    gain_imag = jnp.zeros_like(keep)
    for iteration in range(ITERS):

        def times_step(step, carry, gain_real=gain_real, gain_imag=gain_imag):
            real, imag = load(step)
            mix_real = jnp.sum(real * gain_real + imag * gain_imag, axis=1, keepdims=True)
            mix_imag = jnp.sum(real * gain_imag - imag * gain_real, axis=1, keepdims=True)
            return (
                carry[0] + fold(real * mix_real - imag * mix_imag),
                carry[1] + fold(real * mix_imag + imag * mix_real),
            )

        sums = lax.fori_loop(0, steps, times_step, (zeros, zeros))
        num_real = jnp.sum(sums[0], axis=0, keepdims=True) * inverse
        num_imag = jnp.sum(sums[1], axis=0, keepdims=True) * inverse
        num_real = num_real - (diag_real * gain_real - diag_imag * gain_imag)
        num_imag = num_imag - (diag_real * gain_imag + diag_imag * gain_real)
        power = gain_real * gain_real + gain_imag * gain_imag
        denominator = jnp.sum(power, axis=1, keepdims=True) - power
        new_real = keep * num_real / denominator
        new_imag = keep * num_imag / denominator
        if iteration % 2 == 1:
            new_real = 0.5 * (new_real + gain_real)
            new_imag = 0.5 * (new_imag + gain_imag)
        gain_real, gain_imag = new_real, new_imag
    out_ref[0, 0:1, :] = gain_real
    out_ref[0, 1:2, :] = gain_imag


def params():
    return pltpu.CompilerParams(vmem_limit_bytes=VMEM)


def body(voltages, flags):
    row_count = voltages.shape[1]
    frame_count = voltages.shape[2] // NCH
    chan_count = lax.axis_size("chan")
    tile_count = lax.axis_size("tile")
    inputs = row_count * tile_count
    device_count = chan_count * tile_count
    own = NCH // device_count
    pairs = frame_count // 2
    samples = frame_count * chan_count

    history = lax.ppermute(
        voltages[:, :, (frame_count - (TAPS - 1)) * NCH :], "chan", [(c, c + 1) for c in range(chan_count - 1)]
    )
    spectra = pl.pallas_call(
        spectra_kernel,
        out_shape=jax.ShapeDtypeStruct((2 * NCH, pairs, 128), jnp.bfloat16),
        scratch_shapes=[
            pltpu.VMEM((frame_count * row_count, 2 * NCH), jnp.bfloat16),
            pltpu.VMEM((2 * NCH * pairs, 128), jnp.float32),
        ],
        compiler_params=params(),
        name="spectra",
    )(voltages, history, jnp.asarray(taps_table()), jnp.asarray(dft_table(), jnp.bfloat16))

    turned = lax.all_to_all(
        spectra.reshape(device_count, own, 2, pairs, 128), ("chan", "tile"), split_axis=0, concat_axis=0, tiled=True
    )
    turned = turned.reshape(chan_count, tile_count, own, 2, pairs, 128)

    blocks = 4
    vis_shape = jax.ShapeDtypeStruct((tile_count, own, row_count, inputs), jnp.bfloat16)
    vis_spec = pl.BlockSpec((tile_count // blocks, 1, row_count, inputs), lambda a, b: (b, a, 0, 0))
    series_spec = pl.BlockSpec((1, 2 * samples, inputs), lambda a, b: (a, 0, 0))
    series, across, real = pl.pallas_call(
        real_kernel,
        grid=(own, blocks),
        in_specs=[pl.BlockSpec((chan_count, tile_count, 1, 2, pairs, 128), lambda a, b: (0, 0, a, 0, 0, 0))],
        out_specs=[series_spec, pl.BlockSpec((1, inputs, 2 * samples), lambda a, b: (a, 0, 0)), vis_spec],
        out_shape=[
            jax.ShapeDtypeStruct((own, 2 * samples, inputs), jnp.bfloat16),
            jax.ShapeDtypeStruct((own, inputs, 2 * samples), jnp.bfloat16),
            vis_shape,
        ],
        compiler_params=params(),
        name="real_sums",
    )(turned)
    real = lax.all_to_all(real, "tile", split_axis=0, concat_axis=0, tiled=True)
    imag = pl.pallas_call(
        imag_kernel,
        grid=(own, blocks),
        in_specs=[series_spec, pl.BlockSpec((1, inputs // blocks, 2 * samples), lambda a, b: (a, b, 0))],
        out_specs=vis_spec,
        out_shape=vis_shape,
        compiler_params=params(),
        cost_estimate=pl.CostEstimate(flops=2 * own * inputs * inputs * 2 * samples, bytes_accessed=8 << 20, transcendentals=0),
        name="imag_sums",
    )(series, across)
    imag = lax.all_to_all(imag, "tile", split_axis=0, concat_axis=0, tiled=True)

    gains = pl.pallas_call(
        gains_kernel,
        grid=(own,),
        in_specs=[
            pl.BlockSpec((1, 2 * samples, inputs), lambda a: (a, 0, 0)),
            pl.BlockSpec((1, inputs), lambda a: (0, 0)),
        ],
        out_specs=pl.BlockSpec((1, 2, inputs), lambda a: (a, 0, 0)),
        out_shape=jax.ShapeDtypeStruct((own, 2, inputs), jnp.float32),
        compiler_params=params(),
        cost_estimate=pl.CostEstimate(flops=own * inputs * samples * 64, bytes_accessed=2 << 20, transcendentals=0),
        name="gains",
    )(series, flags.reshape(1, inputs))
    gains = gains.reshape(own, 2, tile_count, row_count).transpose(2, 1, 0, 3)
    gains = lax.all_to_all(gains, "tile", split_axis=0, concat_axis=0, tiled=True)
    gains = gains.transpose(1, 0, 2, 3).reshape(2, tile_count * own, row_count)

    channels = tile_count * own
    visibilities = jnp.stack(
        [real.reshape(channels, row_count, inputs), imag.reshape(channels, row_count, inputs)]
    )
    return (visibilities, gains)


def solution(mesh):
    in_specs = (P(None, "tile", "chan"), P())
    out_specs = (P(None, "chan", "tile", None), P(None, "chan", "tile"))
    return jax.shard_map(body, mesh=mesh, in_specs=in_specs, out_specs=out_specs, check_vma=False)
```

```python
import functools
import math

import jax
import jax.numpy as jnp
import numpy as np
from jax import lax
from jax.experimental import pallas as pl
from jax.experimental.pallas import tpu as pltpu
from jax.sharding import PartitionSpec as P

NCH = 256
TAPS = 16
ITERS = 3
SHIFTS = (1, 3, 2, 0)
VMEM = 56 * 1024 * 1024


def taps_table():
    length = TAPS * NCH
    index = np.arange(length, dtype=np.float64)
    centre = (length - 1) / 2.0
    window = 0.5 - 0.5 * np.cos(2.0 * math.pi * (index + 0.5) / length)
    values = np.sinc((index - centre) / NCH) * window
    values = values * np.sqrt(NCH / np.sum(values * values))
    return values.reshape(TAPS, NCH).astype(np.float32)


def dft_table():
    index = np.arange(NCH)
    angle = (2.0 * math.pi / NCH) * (index[:, None] * index[None, :] % NCH)
    scale = 1.0 / math.sqrt(NCH)
    cosine = np.cos(angle) * scale
    sine = np.sin(angle) * scale
    real = np.concatenate([cosine, sine], axis=1)
    imag = np.concatenate([-sine, cosine], axis=1)
    return np.stack([real, imag], axis=1).reshape(2 * NCH, 2 * NCH).astype(np.float32)


def filter_frames(read, taps_ref, x_ref):
    frames = x_ref.shape[0] // 64

    def filter_tile(index, _):
        part = index // 8
        rows = pl.multiple_of((index // 2) % 4 * 16, 16)
        lane = pl.multiple_of(index % 2 * 128, 128)
        taps = [taps_ref[pl.ds(t, 1), pl.ds(lane, 128)] for t in range(TAPS)]
        window = []
        for f in range(frames + TAPS - 1):
            window.append(read(f, part, rows, lane).astype(jnp.float32))
            m = f - (TAPS - 1)
            if m < 0:
                continue
            total = taps[0] * window[m]
            for t in range(1, TAPS):
                total = total + taps[t] * window[m + t]
            x_ref[pl.ds(rows + m * 64, 16), pl.ds(part * NCH + lane, 128)] = total.astype(jnp.bfloat16)
        return 0

    lax.fori_loop(0, 16, filter_tile, 0)


def transform(x_ref, table_ref, wide_ref, store):
    pairs = x_ref.shape[0] // 128
    for block in range(pairs // 2):
        spectra = lax.dot_general(
            table_ref[...],
            x_ref[pl.ds(block * 256, 256), :],
            (((1,), (1,)), ((), ())),
            preferred_element_type=jnp.float32,
        )
        for half in range(2):
            wide_ref[pl.ds(block * 2 + half, 2 * NCH, stride=pairs), :] = spectra[:, half * 128 : half * 128 + 128]

    def narrow(index, _):
        rows = 64 * pairs
        tile = wide_ref[pl.ds(pl.multiple_of(index * rows, rows), rows), :]
        store(pl.multiple_of(index * 16, 16), tile.astype(jnp.bfloat16).reshape(16, 2, 2 * pairs, 128))
        return 0

    lax.fori_loop(0, 8, narrow, 0)


def late_kernel(v_ref, taps_ref, table_ref, out_ref, x_ref, wide_ref):
    first = v_ref.shape[2] // NCH // 2 - (TAPS - 1)

    def read(f, part, rows, lane):
        return v_ref[part, pl.ds(rows, 16), pl.ds(lane + (first + f) * NCH, 128)]

    def store(device, tile):
        out_ref[pl.ds(device, 16)] = tile

    filter_frames(read, taps_ref, x_ref)
    transform(x_ref, table_ref, wide_ref, store)


def early_kernel(v_ref, h_ref, late_ref, taps_ref, table_ref, out_ref, x_ref, wide_ref):
    history = TAPS - 1

    def read(f, part, rows, lane):
        if f < history:
            return h_ref[part, pl.ds(rows, 16), pl.ds(lane + f * NCH, 128)]
        return v_ref[part, pl.ds(rows, 16), pl.ds(lane + (f - history) * NCH, 128)]

    def store(device, tile):
        out_ref[pl.ds(device, 16), 0] = tile
        out_ref[pl.ds(device, 16), 1] = late_ref[pl.ds(device, 16)]

    filter_frames(read, taps_ref, x_ref)
    transform(x_ref, table_ref, wide_ref, store)


def order_kernel(recv_ref, *series_refs):
    chans, tiles, halves, own, sub, _ = recv_ref.shape
    rows = chans * halves * sub // 2
    for channel in range(own):
        for pair in range(tiles // 2):

            def parts(tile):
                both = recv_ref[:, tile, :, channel].astype(jnp.float32)
                both = both.reshape(chans * halves, 2, sub // 2, 128)
                return [both[:, part].reshape(rows, 128).astype(jnp.bfloat16) for part in range(2)]

            first, second = parts(2 * pair), parts(2 * pair + 1)
            lanes = slice(pair * 128, pair * 128 + 128)
            for part in range(2):
                low = jnp.concatenate([first[part][:, :64], second[part][:, :64]], axis=1)
                high = jnp.concatenate([first[part][:, 64:], second[part][:, 64:]], axis=1)
                start = 2 * part * rows
                series_refs[channel][start : start + rows, lanes] = low
                series_refs[channel][start + rows : start + 2 * rows, lanes] = high


def form_sums(series_ref, tiles, outs, slot):
    samples, inputs = series_ref.shape
    rows = inputs // 16
    left = []
    for tile in tiles:
        across = series_ref[:, pl.ds(pl.multiple_of(tile // 2 * 128, 128), 128)].T
        left.append(jnp.where(tile % 2 == 0, across[:rows], across[rows:]))
    left = jnp.concatenate(left, axis=0)
    count = left.shape[0]
    turned = jnp.concatenate([left[:, samples // 2 :], -left[:, : samples // 2]], axis=1)
    both = jnp.concatenate([left, turned], axis=0)
    sums = jnp.dot(both, series_ref[...], preferred_element_type=jnp.float32) * (2.0 / samples)
    for n, out_ref in enumerate(outs):
        for part in range(2):
            start = part * count + n * rows
            out_ref[slot, part] = sums[start : start + rows].astype(jnp.bfloat16)


def row_tiles(position_ref, axis, shifts):
    x, y = position_ref[0] // 4, position_ref[0] % 4
    if axis == 0:
        return [(x + shift) % 4 * 4 + y for shift in shifts]
    return [x * 4 + (y + shift) % 4 for shift in shifts]


def own_kernel(position_ref, first_ref, second_ref, *outs):
    for axis, series_ref in enumerate((first_ref, second_ref)):
        form_sums(series_ref, row_tiles(position_ref, axis, SHIFTS), outs[4 * axis : 4 * axis + 4], 0)


def near_kernel(position_ref, *refs):
    series, outs = refs[:4], refs[12:]
    for axis in range(2):
        tiles = row_tiles(position_ref, axis, SHIFTS)
        for slot in range(2):
            form_sums(series[2 * axis + slot], tiles, outs[4 * axis : 4 * axis + 4], slot)


def far_kernel(shifts, position_ref, *refs):
    halves, outs, series_ref = refs[:4], refs[8:12], refs[12]
    for axis in range(2):
        rows = halves[0].shape[0]
        series_ref[axis, 0:rows, :] = halves[2 * axis][...]
        series_ref[axis, rows : 2 * rows, :] = halves[2 * axis + 1][...]
        tiles = row_tiles(position_ref, axis, shifts)
        form_sums(series_ref.at[axis], tiles, outs[2 * axis : 2 * axis + 2], 0)


def place_kernel(moves, position_ref, *refs):
    out_ref, sems = refs[-2:]
    x, y = position_ref[0] // 4, position_ref[0] % 4
    copies = []
    for (axis, shift), part_ref in zip(moves, refs):
        for slot, step in enumerate((0, 2, 3, 1)):
            if axis == 0:
                owner = (x + 4 - shift) % 4 * 4 + (y + step) % 4
            else:
                owner = (x + step) % 4 * 4 + (y + 4 - shift) % 4
            for part in range(2):
                copy = pltpu.make_async_copy(
                    part_ref.at[slot, part], out_ref.at[part, owner * 2 + axis], sems.at[len(copies)]
                )
                copy.start()
                copies.append(copy)
    for copy in copies:
        copy.wait()


def gains_kernel(first_ref, second_ref, flags_ref, out_ref):
    keep = (1 - flags_ref[...]).astype(jnp.float32)
    for channel, series_ref in enumerate((first_ref, second_ref)):
        gain_real, gain_imag = stefcal(series_ref, keep)
        out_ref[channel, 0:1, :] = gain_real
        out_ref[channel, 1:2, :] = gain_imag


def stefcal(series_ref, keep):
    half = series_ref.shape[0] // 2
    steps = half // 16
    inverse = 2.0 / series_ref.shape[0]

    def load(step):
        start = pl.multiple_of(step * 16, 16)
        real = series_ref[pl.ds(start, 16), :].astype(jnp.float32)
        imag = series_ref[pl.ds(half + start, 16), :].astype(jnp.float32)
        return real, imag

    def fold(value):
        return value[0:8] + value[8:16]

    zeros = jnp.zeros((8, keep.shape[1]), jnp.float32)

    def diagonal_step(step, carry):
        real, imag = load(step)
        return (
            carry[0] + fold(real * real + imag * imag),
            carry[1] + fold(imag * real - real * imag),
        )

    diag = lax.fori_loop(0, steps, diagonal_step, (zeros, zeros), unroll=4)
    diag_real = jnp.sum(diag[0], axis=0, keepdims=True) * inverse
    diag_imag = jnp.sum(diag[1], axis=0, keepdims=True) * inverse

    gain_real = keep
    gain_imag = jnp.zeros_like(keep)
    for iteration in range(ITERS):

        def times_step(step, carry, gain_real=gain_real, gain_imag=gain_imag):
            real, imag = load(step)
            mix_real = jnp.sum(real * gain_real + imag * gain_imag, axis=1, keepdims=True)
            mix_imag = jnp.sum(real * gain_imag - imag * gain_real, axis=1, keepdims=True)
            return (
                carry[0] + fold(real * mix_real - imag * mix_imag),
                carry[1] + fold(real * mix_imag + imag * mix_real),
            )

        sums = lax.fori_loop(0, steps, times_step, (zeros, zeros), unroll=4)
        num_real = jnp.sum(sums[0], axis=0, keepdims=True) * inverse
        num_imag = jnp.sum(sums[1], axis=0, keepdims=True) * inverse
        num_real = num_real - (diag_real * gain_real - diag_imag * gain_imag)
        num_imag = num_imag - (diag_real * gain_imag + diag_imag * gain_real)
        power = gain_real * gain_real + gain_imag * gain_imag
        denominator = jnp.sum(power, axis=1, keepdims=True) - power
        new_real = keep * num_real / denominator
        new_imag = keep * num_imag / denominator
        if iteration % 2 == 1:
            new_real = 0.5 * (new_real + gain_real)
            new_imag = 0.5 * (new_imag + gain_imag)
        gain_real, gain_imag = new_real, new_imag
    return gain_real, gain_imag


def params():
    return pltpu.CompilerParams(vmem_limit_bytes=VMEM)


def cost(flops, size):
    return pl.CostEstimate(flops=int(flops), bytes_accessed=int(size), transcendentals=0)


def turn(value, axis, shift):
    pairs = []
    for x in range(4):
        for y in range(4):
            to = ((x + shift) % 4, y) if axis == 0 else (x, (y + shift) % 4)
            pairs.append((x * 4 + y, to[0] * 4 + to[1]))
    return lax.ppermute(value, "tile", pairs)


def place(position, parts, moves, out_shape, previous=None):
    operands = list(parts) + ([] if previous is None else [previous])
    anywhere = pl.BlockSpec(memory_space=pl.ANY)
    return pl.pallas_call(
        functools.partial(place_kernel, moves),
        in_specs=[pl.BlockSpec(memory_space=pltpu.SMEM)]
        + [pl.BlockSpec(memory_space=pltpu.VMEM)] * len(parts)
        + [anywhere] * (len(operands) - len(parts)),
        out_specs=anywhere,
        out_shape=out_shape,
        scratch_shapes=[pltpu.SemaphoreType.DMA((8 * len(parts),))],
        input_output_aliases={} if previous is None else {len(operands): 0},
        compiler_params=params(),
        cost_estimate=cost(0, len(parts) << 21),
        name="place",
    )(position, *operands)


def body(voltages, flags):
    row_count = voltages.shape[1]
    frame_count = voltages.shape[2] // NCH
    chan_count = lax.axis_size("chan")
    tile_count = lax.axis_size("tile")
    inputs = row_count * tile_count
    device_count = chan_count * tile_count
    own = NCH // device_count
    samples = frame_count * chan_count
    half = frame_count // 2
    sub = half

    taps = jnp.asarray(taps_table())
    table = jnp.asarray(dft_table(), jnp.bfloat16)
    scratch = [
        pltpu.VMEM((half * row_count, 2 * NCH), jnp.bfloat16),
        pltpu.VMEM((NCH * half, 128), jnp.float32),
    ]
    history = lax.ppermute(
        voltages[:, :, (frame_count - (TAPS - 1)) * NCH :], "chan", [(c, c + 1) for c in range(chan_count - 1)]
    )
    late = pl.pallas_call(
        late_kernel,
        out_shape=jax.ShapeDtypeStruct((device_count, own, sub, 128), jnp.bfloat16),
        scratch_shapes=scratch,
        compiler_params=params(),
        cost_estimate=cost(1.5e9, 4 << 20),
        name="late_spectra",
    )(voltages, taps, table)
    spectra = pl.pallas_call(
        early_kernel,
        out_shape=jax.ShapeDtypeStruct((device_count, 2, own, sub, 128), jnp.bfloat16),
        scratch_shapes=scratch,
        compiler_params=params(),
        cost_estimate=cost(1.5e9, 6 << 20),
        name="early_spectra",
    )(voltages, history, late, taps, table)

    turned = lax.all_to_all(spectra, ("chan", "tile"), split_axis=0, concat_axis=0, tiled=True)
    turned = turned.reshape(chan_count, tile_count, 2, own, sub, 128)
    series_shape = jax.ShapeDtypeStruct((2 * samples, inputs), jnp.bfloat16)
    series = pl.pallas_call(
        order_kernel,
        out_shape=[series_shape] * own,
        compiler_params=params(),
        cost_estimate=cost(1e6, 4 << 20),
        name="order",
    )(turned)

    position = lax.axis_index("tile").astype(jnp.int32).reshape(1)
    smem = pl.BlockSpec(memory_space=pltpu.SMEM)
    block_shape = jax.ShapeDtypeStruct((4, 2, row_count, inputs), jnp.bfloat16)
    anywhere = pl.BlockSpec(memory_space=pl.ANY)

    def slots(count, index):
        return pl.BlockSpec((count, 2, row_count, inputs), lambda i: (index, 0, 0, 0))

    def whole(shape):
        return pl.BlockSpec(shape, lambda i: (0,) * len(shape))

    flops = 8 * 4 * row_count * inputs * samples
    up = [turn(series[axis], 1 - axis, 1) for axis in range(2)]
    down = [turn(series[axis], 1 - axis, 3) for axis in range(2)]
    blocks = pl.pallas_call(
        own_kernel,
        grid=(1,),
        in_specs=[smem] + [whole((2 * samples, inputs))] * 2,
        out_specs=[slots(1, 0)] * 8,
        out_shape=[block_shape] * 8,
        compiler_params=params(),
        cost_estimate=cost(2 * flops, 4 << 20),
        name="own_sums",
    )(position, *series)
    gains = pl.pallas_call(
        gains_kernel,
        in_specs=[pl.BlockSpec(memory_space=pltpu.VMEM)] * 3,
        out_specs=pl.BlockSpec(memory_space=pltpu.VMEM),
        out_shape=jax.ShapeDtypeStruct((own, 2, inputs), jnp.float32),
        compiler_params=params(),
        cost_estimate=cost(own * inputs * samples * 64, 2 << 20),
        name="gains",
    )(*series, flags.reshape(1, inputs))
    up, down, blocks, gains = lax.optimization_barrier((up, down, blocks, gains))

    far = []
    for axis in range(2):
        far.append(turn(up[axis][:samples], 1 - axis, 1))
        far.append(turn(down[axis][samples:], 1 - axis, 3))
    blocks = pl.pallas_call(
        near_kernel,
        grid=(1,),
        in_specs=[smem] + [whole((2 * samples, inputs))] * 4 + [anywhere] * 8,
        out_specs=[slots(2, 1)] * 8,
        out_shape=[block_shape] * 8,
        input_output_aliases={5 + n: n for n in range(8)},
        compiler_params=params(),
        cost_estimate=cost(4 * flops, 8 << 20),
        name="near_sums",
    )(position, up[0], down[0], up[1], down[1], *blocks)

    def far_sums(shifts, chosen):
        return pl.pallas_call(
            functools.partial(far_kernel, shifts),
            grid=(1,),
            in_specs=[smem] + [whole((samples, inputs))] * 4 + [anywhere] * 4,
            out_specs=[slots(1, 1)] * 4,
            out_shape=[block_shape] * 4,
            scratch_shapes=[pltpu.VMEM((2, 2 * samples, inputs), jnp.bfloat16)],
            input_output_aliases={5 + n: n for n in range(4)},
            compiler_params=params(),
            cost_estimate=cost(flops, 6 << 20),
            name="far_sums",
        )(position, *far, *chosen)

    two = far_sums((2, 0), [blocks[n] for n in (2, 3, 6, 7)])
    one = far_sums((1, 3), [blocks[n] for n in (0, 1, 4, 5)])
    last = [turn(two[0], 0, 2), turn(two[2], 1, 2)]
    sent = [turn(one[0], 0, 1), turn(one[1], 0, 3), turn(one[2], 1, 1), turn(one[3], 1, 3)]

    out_shape = jax.ShapeDtypeStruct((2, tile_count * own, row_count, inputs), jnp.bfloat16)
    visibilities = place(position, [two[1], two[3]], [(0, 0), (1, 0)], out_shape)
    visibilities = place(position, last, [(0, 2), (1, 2)], out_shape, visibilities)
    visibilities = place(position, sent[:3], [(0, 1), (0, 3), (1, 1)], out_shape, visibilities)
    visibilities = place(position, sent[3:], [(1, 3)], out_shape, visibilities)

    gains = gains.reshape(own, 2, tile_count, row_count).transpose(2, 1, 0, 3)
    gains = lax.all_to_all(gains, "tile", split_axis=0, concat_axis=0, tiled=True)
    gains = gains.transpose(1, 0, 2, 3).reshape(2, tile_count * own, row_count)
    return (visibilities, gains)


def solution(mesh):
    in_specs = (P(None, "tile", "chan"), P())
    out_specs = (P(None, "chan", "tile", None), P(None, "chan", "tile"))
    return jax.shard_map(body, mesh=mesh, in_specs=in_specs, out_specs=out_specs, check_vma=False)
```

```python
import functools
import math

import jax
import jax.numpy as jnp
import numpy as np
from jax import lax
from jax.experimental import pallas as pl
from jax.experimental.pallas import tpu as pltpu
from jax.sharding import PartitionSpec as P

NCH = 256
TAPS = 16
ITERS = 3
SHIFTS = (1, 3, 2, 0)
VMEM = 28 * 1024 * 1024


def taps_table():
    length = TAPS * NCH
    index = np.arange(length, dtype=np.float64)
    centre = (length - 1) / 2.0
    window = 0.5 - 0.5 * np.cos(2.0 * math.pi * (index + 0.5) / length)
    values = np.sinc((index - centre) / NCH) * window
    values = values * np.sqrt(NCH / np.sum(values * values))
    return values.reshape(TAPS, NCH).astype(np.float32)


def dft_table():
    index = np.arange(NCH)
    angle = (2.0 * math.pi / NCH) * (index[:, None] * index[None, :] % NCH)
    scale = 1.0 / math.sqrt(NCH)
    cosine = np.cos(angle) * scale
    sine = np.sin(angle) * scale
    real = np.concatenate([cosine, sine], axis=1)
    imag = np.concatenate([-sine, cosine], axis=1)
    return np.stack([real, imag], axis=1).reshape(2 * NCH, 2 * NCH).astype(np.float32)


def filter_frames(read, taps_ref, x_ref):
    frames = x_ref.shape[0] // 64

    def filter_tile(index, _):
        part = index // 8
        rows = pl.multiple_of((index // 2) % 4 * 16, 16)
        lane = pl.multiple_of(index % 2 * 128, 128)
        taps = [taps_ref[pl.ds(t, 1), pl.ds(lane, 128)] for t in range(TAPS)]
        window = []
        for f in range(frames + TAPS - 1):
            window.append(read(f, part, rows, lane).astype(jnp.float32))
            m = f - (TAPS - 1)
            if m < 0:
                continue
            total = taps[0] * window[m]
            for t in range(1, TAPS):
                total = total + taps[t] * window[m + t]
            x_ref[pl.ds(rows + m * 64, 16), pl.ds(part * NCH + lane, 128)] = total.astype(jnp.bfloat16)
        return 0

    lax.fori_loop(0, 16, filter_tile, 0)


def transform(x_ref, table_ref, wide_ref, store):
    pairs = x_ref.shape[0] // 128
    for block in range(pairs // 2):
        spectra = lax.dot_general(
            table_ref[...],
            x_ref[pl.ds(block * 256, 256), :],
            (((1,), (1,)), ((), ())),
            preferred_element_type=jnp.float32,
        )
        for half in range(2):
            wide_ref[pl.ds(block * 2 + half, 2 * NCH, stride=pairs), :] = spectra[:, half * 128 : half * 128 + 128]

    def narrow(index, _):
        rows = 64 * pairs
        tile = wide_ref[pl.ds(pl.multiple_of(index * rows, rows), rows), :]
        store(pl.multiple_of(index * 16, 16), tile.astype(jnp.bfloat16).reshape(16, 2, 2 * pairs, 128))
        return 0

    lax.fori_loop(0, 8, narrow, 0)


def late_kernel(v_ref, taps_ref, table_ref, out_ref, x_ref, wide_ref):
    first = v_ref.shape[2] // NCH // 2 - (TAPS - 1)

    def read(f, part, rows, lane):
        return v_ref[part, pl.ds(rows, 16), pl.ds(lane + (first + f) * NCH, 128)]

    def store(device, tile):
        out_ref[pl.ds(device, 16)] = tile

    filter_frames(read, taps_ref, x_ref)
    transform(x_ref, table_ref, wide_ref, store)


def early_kernel(v_ref, h_ref, late_ref, taps_ref, table_ref, out_ref, x_ref, wide_ref):
    history = TAPS - 1

    def read(f, part, rows, lane):
        if f < history:
            return h_ref[part, pl.ds(rows, 16), pl.ds(lane + f * NCH, 128)]
        return v_ref[part, pl.ds(rows, 16), pl.ds(lane + (f - history) * NCH, 128)]

    def store(device, tile):
        out_ref[pl.ds(device, 16), 0] = tile
        out_ref[pl.ds(device, 16), 1] = late_ref[pl.ds(device, 16)]

    filter_frames(read, taps_ref, x_ref)
    transform(x_ref, table_ref, wide_ref, store)


def order_kernel(recv_ref, series_ref):
    chans, tiles, halves, _, sub, _ = recv_ref.shape
    rows = chans * halves * sub // 2
    for pair in range(tiles // 2):

        def parts(tile):
            both = recv_ref[:, tile, :, 0].astype(jnp.float32)
            both = both.reshape(chans * halves, 2, sub // 2, 128)
            return [both[:, part].reshape(rows, 128).astype(jnp.bfloat16) for part in range(2)]

        first, second = parts(2 * pair), parts(2 * pair + 1)
        lanes = slice(pair * 128, pair * 128 + 128)
        for part in range(2):
            low = jnp.concatenate([first[part][:, :64], second[part][:, :64]], axis=1)
            high = jnp.concatenate([first[part][:, 64:], second[part][:, 64:]], axis=1)
            start = 2 * part * rows
            series_ref[start : start + rows, lanes] = low
            series_ref[start + rows : start + 2 * rows, lanes] = high


def form_sums(series_refs, tiles, outs, slot):
    inputs = series_refs[0].shape[1]
    samples = len(series_refs) * series_refs[0].shape[0] // 2
    rows = inputs // 16
    left = []
    for tile in tiles:
        lanes = pl.ds(pl.multiple_of(tile // 2 * 128, 128), 128)
        across = jnp.concatenate([ref[:, lanes].T for ref in series_refs], axis=1)
        left.append(jnp.where(tile % 2 == 0, across[:rows], across[rows:]))
    left = jnp.concatenate(left, axis=0)
    turned = jnp.concatenate([left[:, samples:], -left[:, :samples]], axis=1)
    both = jnp.concatenate([left, turned], axis=0)
    sums, start = 0.0, 0
    for ref in series_refs:
        depth = ref.shape[0]
        sums = sums + jnp.dot(both[:, start : start + depth], ref[...], preferred_element_type=jnp.float32)
        start += depth
    sums = sums * (1.0 / samples)
    count = left.shape[0]
    for n, out_ref in enumerate(outs):
        for part in range(2):
            start = part * count + n * rows
            out_ref[slot, part] = sums[start : start + rows].astype(jnp.bfloat16)


def row_tiles(position_ref, axis, shifts):
    x, y = position_ref[0] // 4, position_ref[0] % 4
    if axis == 0:
        return [(x + shift) % 4 * 4 + y for shift in shifts]
    return [x * 4 + (y + shift) % 4 for shift in shifts]


def split_kernel(*refs):
    rows = refs[4].shape[0]
    for n in range(4):
        start = n % 2 * rows
        refs[4 + n][...] = refs[n][start : start + rows, :]


def main_kernel(position_ref, *refs):
    series, outs = refs[:6], refs[6:]
    for axis in range(2):
        tiles = row_tiles(position_ref, axis, SHIFTS)
        for slot in range(3):
            form_sums([series[3 * axis + slot]], tiles, outs[4 * axis : 4 * axis + 4], slot)


def far_kernel(position_ref, *refs):
    halves, blocks, outs = refs[:4], refs[4:12], refs[12:]
    for axis in range(2):
        tiles = row_tiles(position_ref, axis, SHIFTS)
        form_sums(halves[2 * axis : 2 * axis + 2], tiles, outs[4 * axis : 4 * axis + 4], 3)
    for block_ref, out_ref in zip(blocks, outs):
        out_ref[0:3] = block_ref[...]


def place_kernel(moves, position_ref, *refs):
    out_ref, held, in_sems, out_sems = refs[-2 - len(moves) - 1], refs[-2 - len(moves) : -2], refs[-2], refs[-1]
    x, y = position_ref[0] // 4, position_ref[0] % 4
    loads = []
    for n, part_ref in enumerate(refs[: len(moves)]):
        load = pltpu.make_async_copy(part_ref, held[n], in_sems.at[n])
        load.start()
        loads.append(load)
    copies = []
    for n, (axis, shift) in enumerate(moves):
        loads[n].wait()
        for slot, step in enumerate((3, 1, 0, 2)):
            if axis == 0:
                owner = (x + 4 - shift) % 4 * 4 + (y + step) % 4
            else:
                owner = (x + step) % 4 * 4 + (y + 4 - shift) % 4
            for part in range(2):
                copy = pltpu.make_async_copy(
                    held[n].at[slot, part], out_ref.at[part, owner * 2 + axis], out_sems.at[len(copies)]
                )
                copy.start()
                copies.append(copy)
    for copy in copies:
        copy.wait()


def gains_kernel(first_ref, second_ref, flags_ref, out_ref):
    keep = (1 - flags_ref[...]).astype(jnp.float32)
    out_ref[...] = jnp.zeros_like(out_ref)
    for channel, series_ref in enumerate((first_ref, second_ref)):
        for part, gain in enumerate(stefcal(series_ref, keep)):
            for tile in range(16):
                place = part * 2 + channel
                out_ref[tile, place : place + 1, 0:64] = gain[:, tile * 64 : tile * 64 + 64]


def stefcal(series_ref, keep):
    half = series_ref.shape[0] // 2
    steps = half // 16
    inverse = 2.0 / series_ref.shape[0]

    def load(step):
        start = pl.multiple_of(step * 16, 16)
        real = series_ref[pl.ds(start, 16), :].astype(jnp.float32)
        imag = series_ref[pl.ds(half + start, 16), :].astype(jnp.float32)
        return real, imag

    def fold(value):
        return value[0:8] + value[8:16]

    zeros = jnp.zeros((8, keep.shape[1]), jnp.float32)

    def diagonal_step(step, carry):
        real, imag = load(step)
        return (
            carry[0] + fold(real * real + imag * imag),
            carry[1] + fold(imag * real - real * imag),
        )

    diag = lax.fori_loop(0, steps, diagonal_step, (zeros, zeros), unroll=4)
    diag_real = jnp.sum(diag[0], axis=0, keepdims=True) * inverse
    diag_imag = jnp.sum(diag[1], axis=0, keepdims=True) * inverse

    gain_real = keep
    gain_imag = jnp.zeros_like(keep)
    for iteration in range(ITERS):

        def times_step(step, carry, gain_real=gain_real, gain_imag=gain_imag):
            real, imag = load(step)
            mix_real = jnp.sum(real * gain_real + imag * gain_imag, axis=1, keepdims=True)
            mix_imag = jnp.sum(real * gain_imag - imag * gain_real, axis=1, keepdims=True)
            return (
                carry[0] + fold(real * mix_real - imag * mix_imag),
                carry[1] + fold(real * mix_imag + imag * mix_real),
            )

        sums = lax.fori_loop(0, steps, times_step, (zeros, zeros), unroll=4)
        num_real = jnp.sum(sums[0], axis=0, keepdims=True) * inverse
        num_imag = jnp.sum(sums[1], axis=0, keepdims=True) * inverse
        num_real = num_real - (diag_real * gain_real - diag_imag * gain_imag)
        num_imag = num_imag - (diag_real * gain_imag + diag_imag * gain_real)
        power = gain_real * gain_real + gain_imag * gain_imag
        denominator = jnp.sum(power, axis=1, keepdims=True) - power
        new_real = keep * num_real / denominator
        new_imag = keep * num_imag / denominator
        if iteration % 2 == 1:
            new_real = 0.5 * (new_real + gain_real)
            new_imag = 0.5 * (new_imag + gain_imag)
        gain_real, gain_imag = new_real, new_imag
    return gain_real, gain_imag


def params():
    return pltpu.CompilerParams(vmem_limit_bytes=VMEM)


def cost(flops, size):
    return pl.CostEstimate(flops=int(flops), bytes_accessed=int(size), transcendentals=0)


def turn(value, axis, shift):
    pairs = []
    for x in range(4):
        for y in range(4):
            to = ((x + shift) % 4, y) if axis == 0 else (x, (y + shift) % 4)
            pairs.append((x * 4 + y, to[0] * 4 + to[1]))
    return lax.ppermute(value, "tile", pairs)


def place(position, parts, moves, out_shape, previous=None):
    operands = list(parts) + ([] if previous is None else [previous])
    anywhere = pl.BlockSpec(memory_space=pl.ANY)
    return pl.pallas_call(
        functools.partial(place_kernel, moves),
        in_specs=[pl.BlockSpec(memory_space=pltpu.SMEM)] + [anywhere] * len(operands),
        out_specs=anywhere,
        out_shape=out_shape,
        scratch_shapes=[pltpu.VMEM(part.shape, part.dtype) for part in parts]
        + [
            pltpu.SemaphoreType.DMA((len(parts),)),
            pltpu.SemaphoreType.DMA((8 * len(parts),)),
        ],
        input_output_aliases={} if previous is None else {len(operands): 0},
        compiler_params=params(),
        cost_estimate=cost(0, len(parts) << 21),
        name="place",
    )(position, *operands)


def body(voltages, flags):
    row_count = voltages.shape[1]
    frame_count = voltages.shape[2] // NCH
    chan_count = lax.axis_size("chan")
    tile_count = lax.axis_size("tile")
    inputs = row_count * tile_count
    device_count = chan_count * tile_count
    own = NCH // device_count
    samples = frame_count * chan_count
    half = frame_count // 2
    sub = half

    taps = jnp.asarray(taps_table())
    table = jnp.asarray(dft_table(), jnp.bfloat16)
    scratch = [
        pltpu.VMEM((half * row_count, 2 * NCH), jnp.bfloat16),
        pltpu.VMEM((NCH * half, 128), jnp.float32),
    ]
    history = lax.ppermute(
        voltages[:, :, (frame_count - (TAPS - 1)) * NCH :], "chan", [(c, c + 1) for c in range(chan_count - 1)]
    )
    late = pl.pallas_call(
        late_kernel,
        out_shape=jax.ShapeDtypeStruct((device_count, own, sub, 128), jnp.bfloat16),
        scratch_shapes=scratch,
        compiler_params=params(),
        cost_estimate=cost(1.5e9, 4 << 20),
        name="late_spectra",
    )(voltages, taps, table)
    spectra = pl.pallas_call(
        early_kernel,
        out_shape=jax.ShapeDtypeStruct((device_count, 2, own, sub, 128), jnp.bfloat16),
        scratch_shapes=scratch,
        compiler_params=params(),
        cost_estimate=cost(1.5e9, 6 << 20),
        name="early_spectra",
    )(voltages, history, late, taps, table)

    turned = lax.all_to_all(spectra, ("chan", "tile"), split_axis=0, concat_axis=0, tiled=True)
    turned = turned.reshape(chan_count, tile_count, 2, own, sub, 128)
    series = [
        pl.pallas_call(
            order_kernel,
            grid=(1,),
            in_specs=[
                pl.BlockSpec(
                    (chan_count, tile_count, 2, 1, sub, 128), lambda i, channel=channel: (0, 0, 0, channel, 0, 0)
                )
            ],
            out_specs=pl.BlockSpec((2 * samples, inputs), lambda i: (0, 0)),
            out_shape=jax.ShapeDtypeStruct((2 * samples, inputs), jnp.bfloat16),
            compiler_params=params(),
            cost_estimate=cost(1e6, 2 << 20),
            name="order",
        )(turned)
        for channel in range(own)
    ]

    position = lax.axis_index("tile").astype(jnp.int32).reshape(1)
    smem = pl.BlockSpec(memory_space=pltpu.SMEM)
    vmem = pl.BlockSpec(memory_space=pltpu.VMEM)
    flops = 8 * 4 * row_count * inputs * samples
    up = [turn(series[axis], 1 - axis, 1) for axis in range(2)]
    down = [turn(series[axis], 1 - axis, 3) for axis in range(2)]
    gains = pl.pallas_call(
        gains_kernel,
        in_specs=[vmem] * 3,
        out_specs=vmem,
        out_shape=jax.ShapeDtypeStruct((tile_count, 8, 128), jnp.float32),
        compiler_params=params(),
        cost_estimate=cost(own * inputs * samples * 64, 2 << 20),
        name="gains",
    )(*series, flags.reshape(1, inputs))
    gains = lax.all_to_all(gains, "tile", split_axis=0, concat_axis=0, tiled=True)
    up, down, gains = lax.optimization_barrier((up, down, gains))
    half_shape = jax.ShapeDtypeStruct((samples, inputs), jnp.bfloat16)
    parts = pl.pallas_call(
        split_kernel,
        in_specs=[vmem] * 4,
        out_specs=[vmem] * 4,
        out_shape=[half_shape] * 4,
        compiler_params=params(),
        cost_estimate=cost(0, 4 << 20),
        name="split",
    )(up[0], down[0], up[1], down[1])
    far = [turn(parts[n], 1 - n // 2, (1, 3)[n % 2]) for n in range(4)]
    blocks = pl.pallas_call(
        main_kernel,
        in_specs=[smem] + [vmem] * 6,
        out_specs=[vmem] * 8,
        out_shape=[jax.ShapeDtypeStruct((3, 2, row_count, inputs), jnp.bfloat16)] * 8,
        compiler_params=params(),
        cost_estimate=cost(6 * flops, 12 << 20),
        name="main_sums",
    )(position, up[0], down[0], series[0], up[1], down[1], series[1])
    blocks = pl.pallas_call(
        far_kernel,
        in_specs=[smem] + [vmem] * 12,
        out_specs=[vmem] * 8,
        out_shape=[jax.ShapeDtypeStruct((4, 2, row_count, inputs), jnp.bfloat16)] * 8,
        compiler_params=params(),
        cost_estimate=cost(2 * flops, 16 << 20),
        name="far_sums",
    )(position, *far, *blocks)

    moves = [(axis, shift) for shift in (2, 1, 3) for axis in range(2)]
    sent = [turn(blocks[4 * axis + SHIFTS.index(shift)], axis, shift) for axis, shift in moves]

    out_shape = jax.ShapeDtypeStruct((2, tile_count * own, row_count, inputs), jnp.bfloat16)
    visibilities = place(position, [blocks[3], blocks[7]], [(0, 0), (1, 0)], out_shape)
    visibilities = place(position, sent, moves, out_shape, visibilities)
    gains = gains[:, : 2 * own, :row_count].reshape(tile_count, 2, own, row_count).transpose(1, 0, 2, 3)
    gains = gains.reshape(2, tile_count * own, row_count)
    return (visibilities, gains)


def solution(mesh):
    in_specs = (P(None, "tile", "chan"), P())
    out_specs = (P(None, "chan", "tile", None), P(None, "chan", "tile"))
    return jax.shard_map(body, mesh=mesh, in_specs=in_specs, out_specs=out_specs, check_vma=False)
```

```python
import functools
import math

import jax
import jax.numpy as jnp
import numpy as np
from jax import lax
from jax.experimental import pallas as pl
from jax.experimental.pallas import tpu as pltpu
from jax.sharding import PartitionSpec as P

NCH = 256
TAPS = 16
ITERS = 3
SHIFTS = (1, 3, 2, 0)


def taps_table():
    length = TAPS * NCH
    index = np.arange(length, dtype=np.float64)
    centre = (length - 1) / 2.0
    window = 0.5 - 0.5 * np.cos(2.0 * math.pi * (index + 0.5) / length)
    values = np.sinc((index - centre) / NCH) * window
    values = values * np.sqrt(NCH / np.sum(values * values))
    return values.reshape(TAPS, NCH).astype(np.float32)


def dft_table():
    index = np.arange(NCH)
    angle = (2.0 * math.pi / NCH) * (index[:, None] * index[None, :] % NCH)
    scale = 1.0 / math.sqrt(NCH)
    cosine = np.cos(angle) * scale
    sine = np.sin(angle) * scale
    real = np.concatenate([cosine, sine], axis=1)
    imag = np.concatenate([-sine, cosine], axis=1)
    return np.stack([real, imag], axis=1).reshape(2 * NCH, 2 * NCH).astype(np.float32)


def filter_frames(read, taps_ref, x_ref):
    frames = x_ref.shape[0] // 64

    def filter_tile(index, _):
        part = index // 8
        rows = pl.multiple_of((index // 2) % 4 * 16, 16)
        lane = pl.multiple_of(index % 2 * 128, 128)
        taps = [taps_ref[pl.ds(t, 1), pl.ds(lane, 128)] for t in range(TAPS)]
        window = []
        for f in range(frames + TAPS - 1):
            window.append(read(f, part, rows, lane).astype(jnp.float32))
            m = f - (TAPS - 1)
            if m < 0:
                continue
            total = taps[0] * window[m]
            for t in range(1, TAPS):
                total = total + taps[t] * window[m + t]
            x_ref[pl.ds(rows + m * 64, 16), pl.ds(part * NCH + lane, 128)] = total.astype(jnp.bfloat16)
        return 0

    lax.fori_loop(0, 16, filter_tile, 0)


def transform(x_ref, table_ref, wide_ref, store):
    pairs = x_ref.shape[0] // 128
    for block in range(pairs // 2):
        spectra = lax.dot_general(
            table_ref[...],
            x_ref[pl.ds(block * 256, 256), :],
            (((1,), (1,)), ((), ())),
            preferred_element_type=jnp.float32,
        )
        for half in range(2):
            wide_ref[pl.ds(block * 2 + half, 2 * NCH, stride=pairs), :] = spectra[:, half * 128 : half * 128 + 128]

    def narrow(index, _):
        rows = 64 * pairs
        tile = wide_ref[pl.ds(pl.multiple_of(index * rows, rows), rows), :]
        store(pl.multiple_of(index * 16, 16), tile.astype(jnp.bfloat16).reshape(16, 2, 2 * pairs, 128))
        return 0

    lax.fori_loop(0, 8, narrow, 0)


def late_kernel(v_ref, taps_ref, table_ref, out_ref, x_ref, wide_ref):
    first = v_ref.shape[2] // NCH // 2 - (TAPS - 1)

    def read(f, part, rows, lane):
        return v_ref[part, pl.ds(rows, 16), pl.ds(lane + (first + f) * NCH, 128)]

    def store(device, tile):
        out_ref[pl.ds(device, 16)] = tile

    filter_frames(read, taps_ref, x_ref)
    transform(x_ref, table_ref, wide_ref, store)


def early_kernel(v_ref, h_ref, late_ref, taps_ref, table_ref, out_ref, x_ref, wide_ref):
    history = TAPS - 1

    def read(f, part, rows, lane):
        if f < history:
            return h_ref[part, pl.ds(rows, 16), pl.ds(lane + f * NCH, 128)]
        return v_ref[part, pl.ds(rows, 16), pl.ds(lane + (f - history) * NCH, 128)]

    def store(device, tile):
        out_ref[pl.ds(device, 16), 0] = tile
        out_ref[pl.ds(device, 16), 1] = late_ref[pl.ds(device, 16)]

    filter_frames(read, taps_ref, x_ref)
    transform(x_ref, table_ref, wide_ref, store)


def order_kernel(recv_ref, real_ref, imag_ref):
    chans, tiles, halves, own, sub, _ = recv_ref.shape
    rows = chans * halves * sub // 2
    for channel in range(own):
        for pair in range(tiles // 2):

            def parts(tile):
                both = recv_ref[:, tile, :, channel].astype(jnp.float32)
                both = both.reshape(chans * halves, 2, sub // 2, 128)
                return [both[:, part].reshape(rows, 128).astype(jnp.bfloat16) for part in range(2)]

            first, second = parts(2 * pair), parts(2 * pair + 1)
            lanes = slice(pair * 128, pair * 128 + 128)
            for part, series_ref in enumerate((real_ref, imag_ref)):
                low = jnp.concatenate([first[part][:, :64], second[part][:, :64]], axis=1)
                high = jnp.concatenate([first[part][:, 64:], second[part][:, 64:]], axis=1)
                series_ref[channel, 0:rows, lanes] = low
                series_ref[channel, rows : 2 * rows, lanes] = high


def form_sums(series_refs, tiles, outs, channel, slot):
    inputs = series_refs[0].shape[1]
    samples = len(series_refs) * series_refs[0].shape[0] // 2
    rows = inputs // 16
    left = []
    for tile in tiles:
        lanes = pl.ds(pl.multiple_of(tile // 2 * 128, 128), 128)
        across = jnp.concatenate([ref[:, lanes].T for ref in series_refs], axis=1)
        left.append(jnp.where(tile % 2 == 0, across[:rows], across[rows:]))
    left = jnp.concatenate(left, axis=0)
    turned = jnp.concatenate([left[:, samples:], -left[:, :samples]], axis=1)
    both = jnp.concatenate([left, turned], axis=0)
    sums, start = 0.0, 0
    for ref in series_refs:
        depth = ref.shape[0]
        sums = sums + jnp.dot(both[:, start : start + depth], ref[...], preferred_element_type=jnp.float32)
        start += depth
    sums = sums * (1.0 / samples)
    count = left.shape[0]
    for n, out_ref in enumerate(outs):
        for part in range(2):
            start = part * count + n * rows
            out_ref[channel, slot, part] = sums[start : start + rows].astype(jnp.bfloat16)


def moved(position_ref, across, along):
    x, y, core = position_ref[0] // 4, position_ref[0] % 4, position_ref[1]
    dx, dy = jnp.where(core == 0, across, along), jnp.where(core == 0, along, across)
    return (x + dx) % 4 * 4 + (y + dy) % 4


def main_kernel(position_ref, *refs):
    series, outs = refs[:6], refs[6:]
    tiles = [moved(position_ref, shift, 0) for shift in SHIFTS]
    for channel in range(2):
        for slot in range(3):
            pieces = [ref.at[channel] for ref in series[2 * slot : 2 * slot + 2]]
            form_sums(pieces, tiles, outs, channel, slot)


def far_kernel(position_ref, *refs):
    series, outs = refs[:2], refs[2:]
    tiles = [moved(position_ref, shift, 0) for shift in SHIFTS]
    for channel in range(2):
        form_sums([ref.at[channel] for ref in series], tiles, outs, channel, 0)


def place_kernel(moves, position_ref, *refs):
    out_ref, out_sems = refs[-2:]
    copies = []
    for n, (shift, steps) in enumerate(moves):
        for channel in range(2):
            for slot, step in enumerate(steps):
                owner = moved(position_ref, 4 - shift, step)
                for part in range(2):
                    copy = pltpu.make_async_copy(
                        refs[n].at[channel, slot, part],
                        out_ref.at[part, owner * 2 + channel],
                        out_sems.at[len(copies)],
                    )
                    copy.start()
                    copies.append(copy)
    for copy in copies:
        copy.wait()


def gains_kernel(real_ref, imag_ref, flags_ref, out_ref):
    keep = (1 - flags_ref[...]).astype(jnp.float32)
    out_ref[...] = jnp.zeros_like(out_ref)
    for channel in range(2):
        for part, gain in enumerate(stefcal(real_ref.at[channel], imag_ref.at[channel], keep)):
            for tile in range(16):
                place = part * 2 + channel
                out_ref[tile, place : place + 1, 0:64] = gain[:, tile * 64 : tile * 64 + 64]


def stefcal(real_ref, imag_ref, keep):
    steps = real_ref.shape[0] // 16
    inverse = 1.0 / real_ref.shape[0]

    def load(step):
        start = pl.multiple_of(step * 16, 16)
        real = real_ref[pl.ds(start, 16), :].astype(jnp.float32)
        imag = imag_ref[pl.ds(start, 16), :].astype(jnp.float32)
        return real, imag

    def fold(value):
        return value[0:8] + value[8:16]

    zeros = jnp.zeros((8, keep.shape[1]), jnp.float32)

    def diagonal_step(step, carry):
        real, imag = load(step)
        return (
            carry[0] + fold(real * real + imag * imag),
            carry[1] + fold(imag * real - real * imag),
        )

    diag = lax.fori_loop(0, steps, diagonal_step, (zeros, zeros), unroll=4)
    diag_real = jnp.sum(diag[0], axis=0, keepdims=True) * inverse
    diag_imag = jnp.sum(diag[1], axis=0, keepdims=True) * inverse

    gain_real = keep
    gain_imag = jnp.zeros_like(keep)
    for iteration in range(ITERS):

        def times_step(step, carry, gain_real=gain_real, gain_imag=gain_imag):
            real, imag = load(step)
            mix_real = jnp.sum(real * gain_real + imag * gain_imag, axis=1, keepdims=True)
            mix_imag = jnp.sum(real * gain_imag - imag * gain_real, axis=1, keepdims=True)
            return (
                carry[0] + fold(real * mix_real - imag * mix_imag),
                carry[1] + fold(real * mix_imag + imag * mix_real),
            )

        sums = lax.fori_loop(0, steps, times_step, (zeros, zeros), unroll=4)
        num_real = jnp.sum(sums[0], axis=0, keepdims=True) * inverse
        num_imag = jnp.sum(sums[1], axis=0, keepdims=True) * inverse
        num_real = num_real - (diag_real * gain_real - diag_imag * gain_imag)
        num_imag = num_imag - (diag_real * gain_imag + diag_imag * gain_real)
        power = gain_real * gain_real + gain_imag * gain_imag
        denominator = jnp.sum(power, axis=1, keepdims=True) - power
        new_real = keep * num_real / denominator
        new_imag = keep * num_imag / denominator
        if iteration % 2 == 1:
            new_real = 0.5 * (new_real + gain_real)
            new_imag = 0.5 * (new_imag + gain_imag)
        gain_real, gain_imag = new_real, new_imag
    return gain_real, gain_imag


def params(mib=22):
    return pltpu.CompilerParams(vmem_limit_bytes=mib << 20)


def cost(flops, size):
    return pl.CostEstimate(flops=int(flops), bytes_accessed=int(size), transcendentals=0)


def turn(value, stage, shift):
    pairs = []
    for chan in range(lax.axis_size("chan")):
        for x in range(4):
            for y in range(4):
                to = (x, (y + shift) % 4) if chan % 2 == stage else ((x + shift) % 4, y)
                pairs.append((chan * 16 + x * 4 + y, chan * 16 + to[0] * 4 + to[1]))
    return lax.ppermute(value, ("chan", "tile"), pairs)


def place(position, parts, moves, out_shape, previous=None):
    operands = list(parts) + ([] if previous is None else [previous])
    anywhere = pl.BlockSpec(memory_space=pl.ANY)
    return pl.pallas_call(
        functools.partial(place_kernel, moves),
        in_specs=[pl.BlockSpec(memory_space=pltpu.SMEM)]
        + [pl.BlockSpec(memory_space=pltpu.VMEM)] * len(parts)
        + [anywhere] * (len(operands) - len(parts)),
        out_specs=anywhere,
        out_shape=out_shape,
        scratch_shapes=[pltpu.SemaphoreType.DMA((sum(4 * len(move[1]) for move in moves),))],
        input_output_aliases={} if previous is None else {len(operands): 0},
        compiler_params=params(10),
        cost_estimate=cost(0, len(parts) << 22),
        name="place",
    )(position, *operands)


def body(voltages, flags):
    row_count = voltages.shape[1]
    frame_count = voltages.shape[2] // NCH
    chan_count = lax.axis_size("chan")
    tile_count = lax.axis_size("tile")
    inputs = row_count * tile_count
    device_count = chan_count * tile_count
    own = NCH // device_count
    samples = frame_count * chan_count
    half = frame_count // 2
    sub = half

    taps = jnp.asarray(taps_table())
    table = jnp.asarray(dft_table(), jnp.bfloat16)
    scratch = [
        pltpu.VMEM((half * row_count, 2 * NCH), jnp.bfloat16),
        pltpu.VMEM((NCH * half, 128), jnp.float32),
    ]
    history = lax.ppermute(
        voltages[:, :, (frame_count - (TAPS - 1)) * NCH :], "chan", [(c, c + 1) for c in range(chan_count - 1)]
    )
    late = pl.pallas_call(
        late_kernel,
        out_shape=jax.ShapeDtypeStruct((device_count, own, sub, 128), jnp.bfloat16),
        scratch_shapes=scratch,
        compiler_params=params(),
        cost_estimate=cost(1.5e9, 4 << 20),
        name="late_spectra",
    )(voltages, taps, table)
    spectra = pl.pallas_call(
        early_kernel,
        out_shape=jax.ShapeDtypeStruct((device_count, 2, own, sub, 128), jnp.bfloat16),
        scratch_shapes=scratch,
        compiler_params=params(),
        cost_estimate=cost(1.5e9, 6 << 20),
        name="early_spectra",
    )(voltages, history, late, taps, table)

    turned = lax.all_to_all(spectra, ("chan", "tile"), split_axis=0, concat_axis=0, tiled=True)
    turned = turned.reshape(chan_count, tile_count, 2, own, sub, 128)
    vmem = pl.BlockSpec(memory_space=pltpu.VMEM)
    smem = pl.BlockSpec(memory_space=pltpu.SMEM)
    series_shape = jax.ShapeDtypeStruct((own, samples, inputs), jnp.bfloat16)
    real, imag = pl.pallas_call(
        order_kernel,
        in_specs=[vmem],
        out_specs=[vmem] * 2,
        out_shape=[series_shape] * 2,
        compiler_params=params(),
        cost_estimate=cost(1e6, 4 << 20),
        name="order",
    )(turned)

    position = jnp.stack([lax.axis_index("tile"), lax.axis_index("chan") % 2]).astype(jnp.int32)
    up_real, down_imag = turn(real, 0, 1), turn(imag, 0, 3)
    up_imag, down_real = turn(imag, 0, 1), turn(real, 0, 3)
    far_real, far_imag = turn(up_real, 0, 1), turn(down_imag, 0, 3)
    gains = pl.pallas_call(
        gains_kernel,
        in_specs=[vmem] * 3,
        out_specs=vmem,
        out_shape=jax.ShapeDtypeStruct((tile_count, 8, 128), jnp.float32),
        compiler_params=params(),
        cost_estimate=cost(own * inputs * samples * 64, 2 << 20),
        name="gains",
    )(real, imag, flags.reshape(1, inputs))
    up_imag, down_real, gains = lax.optimization_barrier((up_imag, down_real, gains))

    flops = 8 * 4 * row_count * inputs * samples
    blocks = pl.pallas_call(
        main_kernel,
        in_specs=[smem] + [vmem] * 6,
        out_specs=[vmem] * 4,
        out_shape=[jax.ShapeDtypeStruct((own, 3, 2, row_count, inputs), jnp.bfloat16)] * 4,
        compiler_params=params(),
        cost_estimate=cost(6 * flops, 12 << 20),
        name="main_sums",
    )(position, up_real, up_imag, down_real, down_imag, real, imag)
    blocks, far_real, far_imag = lax.optimization_barrier((blocks, far_real, far_imag))
    far_blocks = pl.pallas_call(
        far_kernel,
        in_specs=[smem] + [vmem] * 2,
        out_specs=[vmem] * 4,
        out_shape=[jax.ShapeDtypeStruct((own, 1, 2, row_count, inputs), jnp.bfloat16)] * 4,
        compiler_params=params(),
        cost_estimate=cost(2 * flops, 4 << 20),
        name="far_sums",
    )(position, far_real, far_imag)

    near, far = (3, 1, 0), (2,)
    order = (1, 3, 2)
    sent = [turn(blocks[SHIFTS.index(shift)], 1, shift) for shift in order]
    sent_far = [turn(far_blocks[SHIFTS.index(shift)], 1, shift) for shift in order]
    out_shape = jax.ShapeDtypeStruct((2, tile_count * own, row_count, inputs), jnp.bfloat16)
    visibilities = place(position, [blocks[3], far_blocks[3]], [(0, near), (0, far)], out_shape)
    gains, sent[0], visibilities = lax.optimization_barrier((gains, sent[0], visibilities))
    gains = lax.all_to_all(gains, "tile", split_axis=0, concat_axis=0, tiled=True)
    moves = [(shift, steps) for steps in (near, far) for shift in order]
    visibilities = place(position, sent + sent_far, moves, out_shape, visibilities)
    gains = gains[:, : 2 * own, :row_count].reshape(tile_count, 2, own, row_count).transpose(1, 0, 2, 3)
    gains = gains.reshape(2, tile_count * own, row_count)
    return (visibilities, gains)


def solution(mesh):
    in_specs = (P(None, "tile", "chan"), P())
    out_specs = (P(None, "chan", "tile", None), P(None, "chan", "tile"))
    return jax.shard_map(body, mesh=mesh, in_specs=in_specs, out_specs=out_specs, check_vma=False)
```

```python
import functools
import math

import jax
import jax.numpy as jnp
import numpy as np
from jax import lax
from jax.experimental import pallas as pl
from jax.experimental.pallas import tpu as pltpu
from jax.sharding import PartitionSpec as P

NCH = 256
TAPS = 16
ITERS = 3
SHIFTS = (1, 3, 2, 0)


def taps_table():
    length = TAPS * NCH
    index = np.arange(length, dtype=np.float64)
    centre = (length - 1) / 2.0
    window = 0.5 - 0.5 * np.cos(2.0 * math.pi * (index + 0.5) / length)
    values = np.sinc((index - centre) / NCH) * window
    values = values * np.sqrt(NCH / np.sum(values * values))
    return values.reshape(TAPS, NCH).astype(np.float32)


def dft_table():
    index = np.arange(NCH)
    angle = (2.0 * math.pi / NCH) * (index[:, None] * index[None, :] % NCH)
    scale = 1.0 / math.sqrt(NCH)
    cosine = np.cos(angle) * scale
    sine = np.sin(angle) * scale
    real = np.concatenate([cosine, sine], axis=1)
    imag = np.concatenate([-sine, cosine], axis=1)
    return np.stack([real, imag], axis=1).reshape(2 * NCH, 2 * NCH).astype(np.float32)


def filter_frames(read, taps_ref, x_ref):
    frames = x_ref.shape[0] // 64

    def filter_tile(index, _):
        part = index // 8
        rows = pl.multiple_of((index // 2) % 4 * 16, 16)
        lane = pl.multiple_of(index % 2 * 128, 128)
        taps = [taps_ref[pl.ds(t, 1), pl.ds(lane, 128)] for t in range(TAPS)]
        window = []
        for f in range(frames + TAPS - 1):
            window.append(read(f, part, rows, lane).astype(jnp.float32))
            m = f - (TAPS - 1)
            if m < 0:
                continue
            total = taps[0] * window[m]
            for t in range(1, TAPS):
                total = total + taps[t] * window[m + t]
            x_ref[pl.ds(rows + m * 64, 16), pl.ds(part * NCH + lane, 128)] = total.astype(jnp.bfloat16)
        return 0

    lax.fori_loop(0, 16, filter_tile, 0)


def transform(x_ref, table_ref, wide_ref, store):
    pairs = x_ref.shape[0] // 128
    for block in range(pairs // 2):
        spectra = lax.dot_general(
            table_ref[...],
            x_ref[pl.ds(block * 256, 256), :],
            (((1,), (1,)), ((), ())),
            preferred_element_type=jnp.float32,
        )
        for half in range(2):
            wide_ref[pl.ds(block * 2 + half, 2 * NCH, stride=pairs), :] = spectra[:, half * 128 : half * 128 + 128]

    def narrow(index, _):
        rows = 64 * pairs
        tile = wide_ref[pl.ds(pl.multiple_of(index * rows, rows), rows), :]
        store(pl.multiple_of(index * 16, 16), tile.astype(jnp.bfloat16).reshape(16, 2, 2 * pairs, 128))
        return 0

    lax.fori_loop(0, 8, narrow, 0)


def late_kernel(v_ref, taps_ref, table_ref, out_ref, x_ref, wide_ref):
    first = v_ref.shape[2] // NCH // 2 - (TAPS - 1)

    def read(f, part, rows, lane):
        return v_ref[part, pl.ds(rows, 16), pl.ds(lane + (first + f) * NCH, 128)]

    def store(device, tile):
        out_ref[pl.ds(device, 16)] = tile

    filter_frames(read, taps_ref, x_ref)
    transform(x_ref, table_ref, wide_ref, store)


def early_kernel(last_ref, v_ref, before_ref, after_ref, late_ref, taps_ref, table_ref, out_ref, x_ref, wide_ref):
    history = TAPS - 1
    frames = v_ref.shape[2] // NCH
    behind = before_ref.shape[2] // NCH
    middle = x_ref.shape[0] // 2
    kept = jnp.where(last_ref[0] == 1, 0.0, 1.0)

    def read_own(f, part, rows, lane):
        if f < behind:
            return before_ref[part, pl.ds(rows, 16), pl.ds(lane + f * NCH, 128)]
        return v_ref[part, pl.ds(rows, 16), pl.ds(lane + (f - behind) * NCH, 128)]

    def read_next(f, part, rows, lane):
        if f < history:
            tile = v_ref[part, pl.ds(rows, 16), pl.ds(lane + (frames - history + f) * NCH, 128)]
            return tile.astype(jnp.float32) * kept
        return after_ref[part, pl.ds(rows, 16), pl.ds(lane + (f - history) * NCH, 128)]

    def store(device, tile):
        out_ref[pl.ds(device, 16), 0] = tile
        out_ref[pl.ds(device, 16), 1] = late_ref[pl.ds(device, 16)]

    filter_frames(read_own, taps_ref, x_ref.at[pl.ds(0, middle)])
    filter_frames(read_next, taps_ref, x_ref.at[pl.ds(middle, middle)])
    transform(x_ref, table_ref, wide_ref, store)


def order_kernel(recv_ref, real_ref, imag_ref):
    chans, tiles, halves, own, sub, _ = recv_ref.shape
    rows = chans * halves * sub // 2
    for channel in range(own):
        for pair in range(tiles // 2):

            def parts(tile):
                both = recv_ref[:, tile, :, channel].astype(jnp.float32)
                both = both.reshape(chans * halves, 2, sub // 2, 128)
                return [both[:, part].reshape(rows, 128).astype(jnp.bfloat16) for part in range(2)]

            first, second = parts(2 * pair), parts(2 * pair + 1)
            lanes = slice(pair * 128, pair * 128 + 128)
            for part, series_ref in enumerate((real_ref, imag_ref)):
                low = jnp.concatenate([first[part][:, :64], second[part][:, :64]], axis=1)
                high = jnp.concatenate([first[part][:, 64:], second[part][:, 64:]], axis=1)
                series_ref[channel, 0:rows, lanes] = low
                series_ref[channel, rows : 2 * rows, lanes] = high


def form_sums(series_refs, tiles, outs, channel, slot):
    inputs = series_refs[0].shape[1]
    samples = len(series_refs) * series_refs[0].shape[0] // 2
    rows = inputs // 16
    left = []
    for tile in tiles:
        lanes = pl.ds(pl.multiple_of(tile // 2 * 128, 128), 128)
        across = jnp.concatenate([ref[:, lanes].T for ref in series_refs], axis=1)
        left.append(jnp.where(tile % 2 == 0, across[:rows], across[rows:]))
    left = jnp.concatenate(left, axis=0)
    turned = jnp.concatenate([left[:, samples:], -left[:, :samples]], axis=1)
    both = jnp.concatenate([left, turned], axis=0)
    sums, start = 0.0, 0
    for ref in series_refs:
        depth = ref.shape[0]
        sums = sums + jnp.dot(both[:, start : start + depth], ref[...], preferred_element_type=jnp.float32)
        start += depth
    sums = sums * (1.0 / samples)
    count = left.shape[0]
    for n, out_ref in enumerate(outs):
        for part in range(2):
            start = part * count + n * rows
            out_ref[channel, slot, part] = sums[start : start + rows].astype(jnp.bfloat16)


def moved(position_ref, across, along):
    x, y, core = position_ref[0] // 4, position_ref[0] % 4, position_ref[1]
    dx, dy = jnp.where(core == 0, across, along), jnp.where(core == 0, along, across)
    return (x + dx) % 4 * 4 + (y + dy) % 4


def main_kernel(position_ref, *refs):
    series, outs = refs[:6], refs[6:]
    tiles = [moved(position_ref, shift, 0) for shift in SHIFTS]
    for channel in range(2):
        for slot in range(3):
            pieces = [ref.at[channel] for ref in series[2 * slot : 2 * slot + 2]]
            form_sums(pieces, tiles, outs, channel, slot)


def far_kernel(position_ref, *refs):
    series, outs = refs[:2], refs[2:]
    tiles = [moved(position_ref, shift, 0) for shift in SHIFTS]
    for channel in range(2):
        form_sums([ref.at[channel] for ref in series], tiles, outs, channel, 0)


def place_kernel(moves, position_ref, *refs):
    out_ref, out_sems = refs[-2:]
    copies = []
    for n, (shift, steps) in enumerate(moves):
        for channel in range(2):
            for slot, step in enumerate(steps):
                owner = moved(position_ref, 4 - shift, step)
                for part in range(2):
                    copy = pltpu.make_async_copy(
                        refs[n].at[channel, slot, part],
                        out_ref.at[part, owner * 2 + channel],
                        out_sems.at[len(copies)],
                    )
                    copy.start()
                    copies.append(copy)
    for copy in copies:
        copy.wait()


def gains_kernel(real_ref, imag_ref, flags_ref, out_ref):
    keep = (1 - flags_ref[...]).astype(jnp.float32)
    out_ref[...] = jnp.zeros_like(out_ref)
    for channel in range(2):
        for part, gain in enumerate(stefcal(real_ref.at[channel], imag_ref.at[channel], keep)):
            for tile in range(16):
                place = part * 2 + channel
                out_ref[tile, place : place + 1, 0:64] = gain[:, tile * 64 : tile * 64 + 64]


def stefcal(real_ref, imag_ref, keep):
    steps = real_ref.shape[0] // 16
    inverse = 1.0 / real_ref.shape[0]

    def load(step):
        start = pl.multiple_of(step * 16, 16)
        real = real_ref[pl.ds(start, 16), :].astype(jnp.float32)
        imag = imag_ref[pl.ds(start, 16), :].astype(jnp.float32)
        return real, imag

    def fold(value):
        return value[0:8] + value[8:16]

    zeros = jnp.zeros((8, keep.shape[1]), jnp.float32)

    def diagonal_step(step, carry):
        real, imag = load(step)
        return (
            carry[0] + fold(real * real + imag * imag),
            carry[1] + fold(imag * real - real * imag),
        )

    diag = lax.fori_loop(0, steps, diagonal_step, (zeros, zeros), unroll=4)
    diag_real = jnp.sum(diag[0], axis=0, keepdims=True) * inverse
    diag_imag = jnp.sum(diag[1], axis=0, keepdims=True) * inverse

    gain_real = keep
    gain_imag = jnp.zeros_like(keep)
    for iteration in range(ITERS):

        def times_step(step, carry, gain_real=gain_real, gain_imag=gain_imag):
            real, imag = load(step)
            mix_real = jnp.sum(real * gain_real + imag * gain_imag, axis=1, keepdims=True)
            mix_imag = jnp.sum(real * gain_imag - imag * gain_real, axis=1, keepdims=True)
            return (
                carry[0] + fold(real * mix_real - imag * mix_imag),
                carry[1] + fold(real * mix_imag + imag * mix_real),
            )

        sums = lax.fori_loop(0, steps, times_step, (zeros, zeros), unroll=4)
        num_real = jnp.sum(sums[0], axis=0, keepdims=True) * inverse
        num_imag = jnp.sum(sums[1], axis=0, keepdims=True) * inverse
        num_real = num_real - (diag_real * gain_real - diag_imag * gain_imag)
        num_imag = num_imag - (diag_real * gain_imag + diag_imag * gain_real)
        power = gain_real * gain_real + gain_imag * gain_imag
        denominator = jnp.sum(power, axis=1, keepdims=True) - power
        new_real = keep * num_real / denominator
        new_imag = keep * num_imag / denominator
        if iteration % 2 == 1:
            new_real = 0.5 * (new_real + gain_real)
            new_imag = 0.5 * (new_imag + gain_imag)
        gain_real, gain_imag = new_real, new_imag
    return gain_real, gain_imag


def params(mib=22):
    return pltpu.CompilerParams(vmem_limit_bytes=mib << 20)


def cost(flops, size):
    return pl.CostEstimate(flops=int(flops), bytes_accessed=int(size), transcendentals=0)


def turn(value, stage, shift):
    pairs = []
    for chan in range(lax.axis_size("chan")):
        for x in range(4):
            for y in range(4):
                to = (x, (y + shift) % 4) if chan % 2 == stage else ((x + shift) % 4, y)
                pairs.append((chan * 16 + x * 4 + y, chan * 16 + to[0] * 4 + to[1]))
    return lax.ppermute(value, ("chan", "tile"), pairs)


def place(position, parts, moves, out_shape, previous=None):
    operands = list(parts) + ([] if previous is None else [previous])
    anywhere = pl.BlockSpec(memory_space=pl.ANY)
    return pl.pallas_call(
        functools.partial(place_kernel, moves),
        in_specs=[pl.BlockSpec(memory_space=pltpu.SMEM)]
        + [pl.BlockSpec(memory_space=pltpu.VMEM)] * len(parts)
        + [anywhere] * (len(operands) - len(parts)),
        out_specs=anywhere,
        out_shape=out_shape,
        scratch_shapes=[pltpu.SemaphoreType.DMA((sum(4 * len(move[1]) for move in moves),))],
        input_output_aliases={} if previous is None else {len(operands): 0},
        compiler_params=params(10),
        cost_estimate=cost(0, len(parts) << 22),
        name="place",
    )(position, *operands)


def body(voltages, flags):
    row_count = voltages.shape[1]
    frame_count = voltages.shape[2] // NCH
    chan_count = lax.axis_size("chan")
    tile_count = lax.axis_size("tile")
    inputs = row_count * tile_count
    device_count = chan_count * tile_count
    own = NCH // device_count
    samples = frame_count * chan_count
    half = frame_count // 2
    sub = half

    taps = jnp.asarray(taps_table())
    table = jnp.asarray(dft_table(), jnp.bfloat16)
    scratch = [
        pltpu.VMEM((half * row_count, 2 * NCH), jnp.bfloat16),
        pltpu.VMEM((NCH * half, 128), jnp.float32),
    ]
    behind = TAPS - 1 - half // 2
    before = lax.ppermute(
        voltages[:, :, (frame_count - behind) * NCH :], "chan", [(c, c + 1) for c in range(chan_count - 1)]
    )
    after = lax.ppermute(
        voltages[:, :, : half // 2 * NCH], "chan", [(c, (c - 1) % chan_count) for c in range(chan_count)]
    )
    last = (lax.axis_index("chan") == chan_count - 1).astype(jnp.int32).reshape(1)
    late = pl.pallas_call(
        late_kernel,
        out_shape=jax.ShapeDtypeStruct((device_count, own, sub, 128), jnp.bfloat16),
        scratch_shapes=scratch,
        compiler_params=params(),
        cost_estimate=cost(1.5e9, 4 << 20),
        name="late_spectra",
    )(voltages, taps, table)
    spectra = pl.pallas_call(
        early_kernel,
        in_specs=[pl.BlockSpec(memory_space=pltpu.SMEM)] + [pl.BlockSpec(memory_space=pltpu.VMEM)] * 6,
        out_shape=jax.ShapeDtypeStruct((device_count, 2, own, sub, 128), jnp.bfloat16),
        scratch_shapes=scratch,
        compiler_params=params(),
        cost_estimate=cost(1.5e9, 6 << 20),
        name="early_spectra",
    )(last, voltages, before, after, late, taps, table)

    turned = lax.all_to_all(spectra, ("chan", "tile"), split_axis=0, concat_axis=0, tiled=True)
    turned = turned.reshape(chan_count, tile_count, 2, own, sub, 128)
    vmem = pl.BlockSpec(memory_space=pltpu.VMEM)
    smem = pl.BlockSpec(memory_space=pltpu.SMEM)
    series_shape = jax.ShapeDtypeStruct((own, samples, inputs), jnp.bfloat16)
    real, imag = pl.pallas_call(
        order_kernel,
        in_specs=[vmem],
        out_specs=[vmem] * 2,
        out_shape=[series_shape] * 2,
        compiler_params=params(),
        cost_estimate=cost(1e6, 4 << 20),
        name="order",
    )(turned)

    position = jnp.stack([lax.axis_index("tile"), lax.axis_index("chan") % 2]).astype(jnp.int32)
    up_real, down_imag = turn(real, 0, 1), turn(imag, 0, 3)
    up_imag, down_real = turn(imag, 0, 1), turn(real, 0, 3)
    far_real, far_imag = turn(up_real, 0, 1), turn(down_imag, 0, 3)
    gains = pl.pallas_call(
        gains_kernel,
        in_specs=[vmem] * 3,
        out_specs=vmem,
        out_shape=jax.ShapeDtypeStruct((tile_count, 8, 128), jnp.float32),
        compiler_params=params(),
        cost_estimate=cost(own * inputs * samples * 64, 2 << 20),
        name="gains",
    )(real, imag, flags.reshape(1, inputs))
    up_imag, down_real, gains = lax.optimization_barrier((up_imag, down_real, gains))

    flops = 8 * 4 * row_count * inputs * samples
    blocks = pl.pallas_call(
        main_kernel,
        in_specs=[smem] + [vmem] * 6,
        out_specs=[vmem] * 4,
        out_shape=[jax.ShapeDtypeStruct((own, 3, 2, row_count, inputs), jnp.bfloat16)] * 4,
        compiler_params=params(),
        cost_estimate=cost(6 * flops, 12 << 20),
        name="main_sums",
    )(position, up_real, up_imag, down_real, down_imag, real, imag)
    blocks, far_real, far_imag = lax.optimization_barrier((blocks, far_real, far_imag))
    far_blocks = pl.pallas_call(
        far_kernel,
        in_specs=[smem] + [vmem] * 2,
        out_specs=[vmem] * 4,
        out_shape=[jax.ShapeDtypeStruct((own, 1, 2, row_count, inputs), jnp.bfloat16)] * 4,
        compiler_params=params(),
        cost_estimate=cost(2 * flops, 4 << 20),
        name="far_sums",
    )(position, far_real, far_imag)

    near, far = (3, 1, 0), (2,)
    order = (1, 3, 2)
    sent = [turn(blocks[SHIFTS.index(shift)], 1, shift) for shift in order]
    sent_far = [turn(far_blocks[SHIFTS.index(shift)], 1, shift) for shift in order]
    out_shape = jax.ShapeDtypeStruct((2, tile_count * own, row_count, inputs), jnp.bfloat16)
    visibilities = place(position, [blocks[3], far_blocks[3]], [(0, near), (0, far)], out_shape)
    gains, sent[0], visibilities = lax.optimization_barrier((gains, sent[0], visibilities))
    gains = lax.all_to_all(gains, "tile", split_axis=0, concat_axis=0, tiled=True)
    moves = [(shift, steps) for steps in (near, far) for shift in order]
    visibilities = place(position, sent + sent_far, moves, out_shape, visibilities)
    gains = gains[:, : 2 * own, :row_count].reshape(tile_count, 2, own, row_count).transpose(1, 0, 2, 3)
    gains = gains.reshape(2, tile_count * own, row_count)
    return (visibilities, gains)


def solution(mesh):
    in_specs = (P(None, "tile", "chan"), P())
    out_specs = (P(None, "chan", "tile", None), P(None, "chan", "tile"))
    return jax.shard_map(body, mesh=mesh, in_specs=in_specs, out_specs=out_specs, check_vma=False)
```

```python
import functools
import math

import jax
import jax.numpy as jnp
import numpy as np
from jax import lax
from jax.experimental import pallas as pl
from jax.experimental.pallas import tpu as pltpu
from jax.sharding import PartitionSpec as P

NCH = 256
TAPS = 16
ITERS = 3
SHIFTS = (1, 3, 2, 0)


def taps_table():
    length = TAPS * NCH
    index = np.arange(length, dtype=np.float64)
    centre = (length - 1) / 2.0
    window = 0.5 - 0.5 * np.cos(2.0 * math.pi * (index + 0.5) / length)
    values = np.sinc((index - centre) / NCH) * window
    values = values * np.sqrt(NCH / np.sum(values * values))
    return values.reshape(TAPS, NCH).astype(np.float32)


def dft_table():
    index = np.arange(NCH)
    angle = (2.0 * math.pi / NCH) * (index[:, None] * index[None, :] % NCH)
    scale = 1.0 / math.sqrt(NCH)
    cosine = np.cos(angle) * scale
    sine = np.sin(angle) * scale
    real = np.concatenate([cosine, sine], axis=1)
    imag = np.concatenate([-sine, cosine], axis=1)
    return np.stack([real, imag], axis=1).reshape(2 * NCH, 2 * NCH).astype(np.float32)


def filter_frames(read, taps_ref, x_ref):
    frames = x_ref.shape[0] // 64

    def filter_tile(index, _):
        part = index // 8
        rows = pl.multiple_of((index // 2) % 4 * 16, 16)
        lane = pl.multiple_of(index % 2 * 128, 128)
        taps = [taps_ref[pl.ds(t, 1), pl.ds(lane, 128)] for t in range(TAPS)]
        window = []
        for f in range(frames + TAPS - 1):
            window.append(read(f, part, rows, lane).astype(jnp.float32))
            m = f - (TAPS - 1)
            if m < 0:
                continue
            total = taps[0] * window[m]
            for t in range(1, TAPS):
                total = total + taps[t] * window[m + t]
            x_ref[pl.ds(rows + m * 64, 16), pl.ds(part * NCH + lane, 128)] = total.astype(jnp.bfloat16)
        return 0

    lax.fori_loop(0, 16, filter_tile, 0)


def transform(x_ref, table_ref, wide_ref, store):
    pairs = x_ref.shape[0] // 128
    for block in range(pairs // 2):
        spectra = lax.dot_general(
            table_ref[...],
            x_ref[pl.ds(block * 256, 256), :],
            (((1,), (1,)), ((), ())),
            preferred_element_type=jnp.float32,
        )
        for half in range(2):
            wide_ref[pl.ds(block * 2 + half, 2 * NCH, stride=pairs), :] = spectra[:, half * 128 : half * 128 + 128]

    def narrow(index, _):
        rows = 64 * pairs
        tile = wide_ref[pl.ds(pl.multiple_of(index * rows, rows), rows), :]
        store(pl.multiple_of(index * 16, 16), tile.astype(jnp.bfloat16).reshape(16, 2, 2 * pairs, 128))
        return 0

    lax.fori_loop(0, 8, narrow, 0)


def late_kernel(v_ref, taps_ref, table_ref, out_ref, x_ref, wide_ref):
    first = v_ref.shape[2] // NCH // 2 - (TAPS - 1)

    def read(f, part, rows, lane):
        return v_ref[part, pl.ds(rows, 16), pl.ds(lane + (first + f) * NCH, 128)]

    def store(device, tile):
        out_ref[pl.ds(device, 16)] = tile

    filter_frames(read, taps_ref, x_ref)
    transform(x_ref, table_ref, wide_ref, store)


def early_kernel(last_ref, v_ref, before_ref, after_ref, late_ref, taps_ref, table_ref, out_ref, x_ref, wide_ref):
    history = TAPS - 1
    frames = v_ref.shape[2] // NCH
    behind = before_ref.shape[2] // NCH
    middle = x_ref.shape[0] // 2
    kept = jnp.where(last_ref[0] == 1, 0.0, 1.0)

    def read_own(f, part, rows, lane):
        if f < behind:
            return before_ref[part, pl.ds(rows, 16), pl.ds(lane + f * NCH, 128)]
        return v_ref[part, pl.ds(rows, 16), pl.ds(lane + (f - behind) * NCH, 128)]

    def read_next(f, part, rows, lane):
        if f < history:
            tile = v_ref[part, pl.ds(rows, 16), pl.ds(lane + (frames - history + f) * NCH, 128)]
            return tile.astype(jnp.float32) * kept
        return after_ref[part, pl.ds(rows, 16), pl.ds(lane + (f - history) * NCH, 128)]

    def store(device, tile):
        out_ref[pl.ds(device, 16), 0] = tile
        out_ref[pl.ds(device, 16), 1] = late_ref[pl.ds(device, 16)]

    filter_frames(read_own, taps_ref, x_ref.at[pl.ds(0, middle)])
    filter_frames(read_next, taps_ref, x_ref.at[pl.ds(middle, middle)])
    transform(x_ref, table_ref, wide_ref, store)


def order_kernel(recv_ref, real_ref, imag_ref):
    chans, tiles, halves, own, sub, _ = recv_ref.shape
    rows = chans * halves * sub // 2
    for channel in range(own):
        for pair in range(tiles // 2):

            def parts(tile):
                both = recv_ref[:, tile, :, channel].astype(jnp.float32)
                both = both.reshape(chans * halves, 2, sub // 2, 128)
                return [both[:, part].reshape(rows, 128).astype(jnp.bfloat16) for part in range(2)]

            first, second = parts(2 * pair), parts(2 * pair + 1)
            lanes = slice(pair * 128, pair * 128 + 128)
            for part, series_ref in enumerate((real_ref, imag_ref)):
                low = jnp.concatenate([first[part][:, :64], second[part][:, :64]], axis=1)
                high = jnp.concatenate([first[part][:, 64:], second[part][:, 64:]], axis=1)
                series_ref[channel, 0:rows, lanes] = low
                series_ref[channel, rows : 2 * rows, lanes] = high


def form_sums(series_refs, tiles, outs, channel, slot):
    inputs = series_refs[0].shape[1]
    samples = len(series_refs) * series_refs[0].shape[0] // 2
    rows = inputs // 16
    left = []
    for tile in tiles:
        lanes = pl.ds(pl.multiple_of(tile // 2 * 128, 128), 128)
        across = jnp.concatenate([ref[:, lanes].T for ref in series_refs], axis=1)
        left.append(jnp.where(tile % 2 == 0, across[:rows], across[rows:]))
    left = jnp.concatenate(left, axis=0)
    turned = jnp.concatenate([left[:, samples:], -left[:, :samples]], axis=1)
    both = jnp.concatenate([left, turned], axis=0)
    sums, start = 0.0, 0
    for ref in series_refs:
        depth = ref.shape[0]
        sums = sums + jnp.dot(both[:, start : start + depth], ref[...], preferred_element_type=jnp.float32)
        start += depth
    sums = sums * (1.0 / samples)
    count = left.shape[0]
    for n, out_ref in enumerate(outs):
        for part in range(2):
            start = part * count + n * rows
            out_ref[channel, slot, part] = sums[start : start + rows].astype(jnp.bfloat16)


def moved(position_ref, across, along):
    x, y, core = position_ref[0] // 4, position_ref[0] % 4, position_ref[1]
    dx, dy = jnp.where(core == 0, across, along), jnp.where(core == 0, along, across)
    return (x + dx) % 4 * 4 + (y + dy) % 4


def main_kernel(position_ref, *refs):
    series, outs = refs[:6], refs[6:]
    tiles = [moved(position_ref, shift, 0) for shift in SHIFTS]
    for channel in range(2):
        for slot in range(3):
            pieces = [ref.at[channel] for ref in series[2 * slot : 2 * slot + 2]]
            form_sums(pieces, tiles, outs, channel, slot)


def far_kernel(position_ref, *refs):
    series, outs = refs[:2], refs[2:]
    tiles = [moved(position_ref, shift, 0) for shift in SHIFTS]
    for channel in range(2):
        form_sums([ref.at[channel] for ref in series], tiles, outs, channel, 0)


def place_kernel(moves, position_ref, *refs):
    out_ref, out_sems = refs[-2:]
    copies = []
    for n, (shift, steps) in enumerate(moves):
        for channel in range(2):
            for slot, step in enumerate(steps):
                owner = moved(position_ref, 4 - shift, step)
                for part in range(2):
                    copy = pltpu.make_async_copy(
                        refs[n].at[channel, slot, part],
                        out_ref.at[part, owner * 2 + channel],
                        out_sems.at[len(copies)],
                    )
                    copy.start()
                    copies.append(copy)
    for copy in copies:
        copy.wait()


def gains_kernel(real_ref, imag_ref, flags_ref, out_ref):
    keep = (1 - flags_ref[...]).astype(jnp.float32)
    out_ref[...] = jnp.zeros_like(out_ref)
    for channel in range(2):
        for part, gain in enumerate(stefcal(real_ref.at[channel], imag_ref.at[channel], keep)):
            for tile in range(16):
                place = part * 2 + channel
                out_ref[tile, place : place + 1, 0:64] = gain[:, tile * 64 : tile * 64 + 64]


def stefcal(real_ref, imag_ref, keep):
    steps = real_ref.shape[0] // 16
    inverse = 1.0 / real_ref.shape[0]

    def load(step):
        start = pl.multiple_of(step * 16, 16)
        real = real_ref[pl.ds(start, 16), :].astype(jnp.float32)
        imag = imag_ref[pl.ds(start, 16), :].astype(jnp.float32)
        return real, imag

    def fold(value):
        return value[0:8] + value[8:16]

    zeros = jnp.zeros((8, keep.shape[1]), jnp.float32)

    def diagonal_step(step, carry):
        real, imag = load(step)
        return (
            carry[0] + fold(real * real + imag * imag),
            carry[1] + fold(imag * real - real * imag),
        )

    diag = lax.fori_loop(0, steps, diagonal_step, (zeros, zeros), unroll=4)
    diag_real = jnp.sum(diag[0], axis=0, keepdims=True) * inverse
    diag_imag = jnp.sum(diag[1], axis=0, keepdims=True) * inverse

    gain_real = keep
    gain_imag = jnp.zeros_like(keep)
    for iteration in range(ITERS):

        def times_step(step, carry, gain_real=gain_real, gain_imag=gain_imag):
            real, imag = load(step)
            mix_real = jnp.sum(real * gain_real + imag * gain_imag, axis=1, keepdims=True)
            mix_imag = jnp.sum(real * gain_imag - imag * gain_real, axis=1, keepdims=True)
            return (
                carry[0] + fold(real * mix_real - imag * mix_imag),
                carry[1] + fold(real * mix_imag + imag * mix_real),
            )

        sums = lax.fori_loop(0, steps, times_step, (zeros, zeros), unroll=4)
        num_real = jnp.sum(sums[0], axis=0, keepdims=True) * inverse
        num_imag = jnp.sum(sums[1], axis=0, keepdims=True) * inverse
        num_real = num_real - (diag_real * gain_real - diag_imag * gain_imag)
        num_imag = num_imag - (diag_real * gain_imag + diag_imag * gain_real)
        power = gain_real * gain_real + gain_imag * gain_imag
        denominator = jnp.sum(power, axis=1, keepdims=True) - power
        new_real = keep * num_real / denominator
        new_imag = keep * num_imag / denominator
        if iteration % 2 == 1:
            new_real = 0.5 * (new_real + gain_real)
            new_imag = 0.5 * (new_imag + gain_imag)
        gain_real, gain_imag = new_real, new_imag
    return gain_real, gain_imag


def params(mib=22):
    return pltpu.CompilerParams(vmem_limit_bytes=mib << 20)


def cost(flops, size):
    return pl.CostEstimate(flops=int(flops), bytes_accessed=int(size), transcendentals=0)


def turn(value, stage, shift):
    pairs = []
    for chan in range(lax.axis_size("chan")):
        for x in range(4):
            for y in range(4):
                to = (x, (y + shift) % 4) if chan % 2 == stage else ((x + shift) % 4, y)
                pairs.append((chan * 16 + x * 4 + y, chan * 16 + to[0] * 4 + to[1]))
    return lax.ppermute(value, ("chan", "tile"), pairs)


def place(position, parts, moves, out_shape, previous=None):
    operands = list(parts) + ([] if previous is None else [previous])
    anywhere = pl.BlockSpec(memory_space=pl.ANY)
    return pl.pallas_call(
        functools.partial(place_kernel, moves),
        in_specs=[pl.BlockSpec(memory_space=pltpu.SMEM)]
        + [pl.BlockSpec(memory_space=pltpu.VMEM)] * len(parts)
        + [anywhere] * (len(operands) - len(parts)),
        out_specs=anywhere,
        out_shape=out_shape,
        scratch_shapes=[pltpu.SemaphoreType.DMA((sum(4 * len(move[1]) for move in moves),))],
        input_output_aliases={} if previous is None else {len(operands): 0},
        compiler_params=params(10),
        cost_estimate=cost(0, len(parts) << 22),
        name="place",
    )(position, *operands)


def body(voltages, flags):
    row_count = voltages.shape[1]
    frame_count = voltages.shape[2] // NCH
    chan_count = lax.axis_size("chan")
    tile_count = lax.axis_size("tile")
    inputs = row_count * tile_count
    device_count = chan_count * tile_count
    own = NCH // device_count
    samples = frame_count * chan_count
    half = frame_count // 2
    sub = half

    taps = jnp.asarray(taps_table())
    table = jnp.asarray(dft_table(), jnp.bfloat16)
    scratch = [
        pltpu.VMEM((half * row_count, 2 * NCH), jnp.bfloat16),
        pltpu.VMEM((NCH * half, 128), jnp.float32),
    ]
    behind = TAPS - 1 - half // 2
    before = lax.ppermute(
        voltages[:, :, (frame_count - behind) * NCH :], "chan", [(c, c + 1) for c in range(chan_count - 1)]
    )
    after = lax.ppermute(
        voltages[:, :, : half // 2 * NCH], "chan", [(c, (c - 1) % chan_count) for c in range(chan_count)]
    )
    last = (lax.axis_index("chan") == chan_count - 1).astype(jnp.int32).reshape(1)
    late = pl.pallas_call(
        late_kernel,
        out_shape=jax.ShapeDtypeStruct((device_count, own, sub, 128), jnp.bfloat16),
        scratch_shapes=scratch,
        compiler_params=params(),
        cost_estimate=cost(1.5e9, 4 << 20),
        name="late_spectra",
    )(voltages, taps, table)
    spectra = pl.pallas_call(
        early_kernel,
        in_specs=[pl.BlockSpec(memory_space=pltpu.SMEM)] + [pl.BlockSpec(memory_space=pltpu.VMEM)] * 6,
        out_shape=jax.ShapeDtypeStruct((device_count, 2, own, sub, 128), jnp.bfloat16),
        scratch_shapes=scratch,
        compiler_params=params(),
        cost_estimate=cost(1.5e9, 6 << 20),
        name="early_spectra",
    )(last, voltages, before, after, late, taps, table)

    turned = lax.all_to_all(spectra, ("chan", "tile"), split_axis=0, concat_axis=0, tiled=True)
    turned = turned.reshape(chan_count, tile_count, 2, own, sub, 128)
    vmem = pl.BlockSpec(memory_space=pltpu.VMEM)
    smem = pl.BlockSpec(memory_space=pltpu.SMEM)
    series_shape = jax.ShapeDtypeStruct((own, samples, inputs), jnp.bfloat16)
    real, imag = pl.pallas_call(
        order_kernel,
        in_specs=[vmem],
        out_specs=[vmem] * 2,
        out_shape=[series_shape] * 2,
        compiler_params=params(),
        cost_estimate=cost(1e6, 4 << 20),
        name="order",
    )(turned)

    position = jnp.stack([lax.axis_index("tile"), lax.axis_index("chan") % 2]).astype(jnp.int32)
    up_real, down_imag = turn(real, 0, 1), turn(imag, 0, 3)
    up_imag, down_real = turn(imag, 0, 1), turn(real, 0, 3)
    far_real, far_imag = turn(up_real, 0, 1), turn(down_imag, 0, 3)
    gains = pl.pallas_call(
        gains_kernel,
        in_specs=[vmem] * 3,
        out_specs=vmem,
        out_shape=jax.ShapeDtypeStruct((tile_count, 8, 128), jnp.float32),
        compiler_params=params(),
        cost_estimate=cost(own * inputs * samples * 64, 2 << 20),
        name="gains",
    )(real, imag, flags.reshape(1, inputs))
    up_imag, down_real, gains = lax.optimization_barrier((up_imag, down_real, gains))

    flops = 8 * 4 * row_count * inputs * samples
    blocks = pl.pallas_call(
        main_kernel,
        in_specs=[smem] + [vmem] * 6,
        out_specs=[vmem] * 4,
        out_shape=[jax.ShapeDtypeStruct((own, 3, 2, row_count, inputs), jnp.bfloat16)] * 4,
        compiler_params=params(),
        cost_estimate=cost(6 * flops, 12 << 20),
        name="main_sums",
    )(position, up_real, up_imag, down_real, down_imag, real, imag)
    blocks, far_real, far_imag = lax.optimization_barrier((blocks, far_real, far_imag))
    far_blocks = pl.pallas_call(
        far_kernel,
        in_specs=[smem] + [vmem] * 2,
        out_specs=[vmem] * 4,
        out_shape=[jax.ShapeDtypeStruct((own, 1, 2, row_count, inputs), jnp.bfloat16)] * 4,
        compiler_params=params(),
        cost_estimate=cost(2 * flops, 4 << 20),
        name="far_sums",
    )(position, far_real, far_imag)

    near, far = (3, 1, 0), (2,)
    order = (1, 3, 2)
    sent = [turn(blocks[SHIFTS.index(shift)], 1, shift) for shift in order]
    sent_far = [turn(far_blocks[SHIFTS.index(shift)], 1, shift) for shift in order]
    out_shape = jax.ShapeDtypeStruct((2, tile_count * own, row_count, inputs), jnp.bfloat16)
    visibilities = place(position, [blocks[3], far_blocks[3]], [(0, near), (0, far)], out_shape)
    gains, sent[1], visibilities = lax.optimization_barrier((gains, sent[1], visibilities))
    gains = lax.all_to_all(gains, "tile", split_axis=0, concat_axis=0, tiled=True)
    moves = [(shift, steps) for steps in (near, far) for shift in order]
    visibilities = place(position, sent + sent_far, moves, out_shape, visibilities)
    gains = gains[:, : 2 * own, :row_count].reshape(tile_count, 2, own, row_count).transpose(1, 0, 2, 3)
    gains = gains.reshape(2, tile_count * own, row_count)
    return (visibilities, gains)


def solution(mesh):
    in_specs = (P(None, "tile", "chan"), P())
    out_specs = (P(None, "chan", "tile", None), P(None, "chan", "tile"))
    return jax.shard_map(body, mesh=mesh, in_specs=in_specs, out_specs=out_specs, check_vma=False)
```

```python
import functools
import math

import jax
import jax.numpy as jnp
import numpy as np
from jax import lax
from jax.experimental import pallas as pl
from jax.experimental.pallas import tpu as pltpu
from jax.sharding import PartitionSpec as P

NCH = 256
TAPS = 16
ITERS = 3
SHIFTS = (1, 3, 2, 0)


def taps_table():
    length = TAPS * NCH
    index = np.arange(length, dtype=np.float64)
    centre = (length - 1) / 2.0
    window = 0.5 - 0.5 * np.cos(2.0 * math.pi * (index + 0.5) / length)
    values = np.sinc((index - centre) / NCH) * window
    values = values * np.sqrt(NCH / np.sum(values * values))
    return values.reshape(TAPS, NCH).astype(np.float32)


def dft_table():
    index = np.arange(NCH)
    angle = (2.0 * math.pi / NCH) * (index[:, None] * index[None, :] % NCH)
    scale = 1.0 / math.sqrt(NCH)
    cosine = np.cos(angle) * scale
    sine = np.sin(angle) * scale
    real = np.concatenate([cosine, sine], axis=1)
    imag = np.concatenate([-sine, cosine], axis=1)
    return np.stack([real, imag], axis=1).reshape(2 * NCH, 2 * NCH).astype(np.float32)


def filter_frames(read, taps_ref, x_ref):
    frames = x_ref.shape[0] // 64

    def filter_tile(index, _):
        part = index // 8
        rows = pl.multiple_of((index // 2) % 4 * 16, 16)
        lane = pl.multiple_of(index % 2 * 128, 128)
        taps = [taps_ref[pl.ds(t, 1), pl.ds(lane, 128)] for t in range(TAPS)]
        window = []
        for f in range(frames + TAPS - 1):
            window.append(read(f, part, rows, lane).astype(jnp.float32))
            m = f - (TAPS - 1)
            if m < 0:
                continue
            total = taps[0] * window[m]
            for t in range(1, TAPS):
                total = total + taps[t] * window[m + t]
            x_ref[pl.ds(rows + m * 64, 16), pl.ds(part * NCH + lane, 128)] = total.astype(jnp.bfloat16)
        return 0

    lax.fori_loop(0, 16, filter_tile, 0)


def transform(x_ref, table_ref, wide_ref, store):
    pairs = x_ref.shape[0] // 128
    for block in range(pairs // 2):
        spectra = lax.dot_general(
            table_ref[...],
            x_ref[pl.ds(block * 256, 256), :],
            (((1,), (1,)), ((), ())),
            preferred_element_type=jnp.float32,
        )
        for half in range(2):
            wide_ref[pl.ds(block * 2 + half, 2 * NCH, stride=pairs), :] = spectra[:, half * 128 : half * 128 + 128]

    def narrow(index, _):
        rows = 64 * pairs
        tile = wide_ref[pl.ds(pl.multiple_of(index * rows, rows), rows), :]
        store(pl.multiple_of(index * 16, 16), tile.astype(jnp.bfloat16).reshape(16, 2, 2 * pairs, 128))
        return 0

    lax.fori_loop(0, 8, narrow, 0)


def late_kernel(v_ref, taps_ref, table_ref, out_ref, x_ref, wide_ref):
    first = v_ref.shape[2] // NCH // 2 - (TAPS - 1)

    def read(f, part, rows, lane):
        return v_ref[part, pl.ds(rows, 16), pl.ds(lane + (first + f) * NCH, 128)]

    def store(device, tile):
        out_ref[pl.ds(device, 16)] = tile

    filter_frames(read, taps_ref, x_ref)
    transform(x_ref, table_ref, wide_ref, store)


def early_kernel(last_ref, v_ref, before_ref, after_ref, late_ref, taps_ref, table_ref, out_ref, x_ref, wide_ref):
    history = TAPS - 1
    frames = v_ref.shape[2] // NCH
    behind = before_ref.shape[2] // NCH
    middle = x_ref.shape[0] // 2
    kept = jnp.where(last_ref[0] == 1, 0.0, 1.0)

    def read_own(f, part, rows, lane):
        if f < behind:
            return before_ref[part, pl.ds(rows, 16), pl.ds(lane + f * NCH, 128)]
        return v_ref[part, pl.ds(rows, 16), pl.ds(lane + (f - behind) * NCH, 128)]

    def read_next(f, part, rows, lane):
        if f < history:
            tile = v_ref[part, pl.ds(rows, 16), pl.ds(lane + (frames - history + f) * NCH, 128)]
            return tile.astype(jnp.float32) * kept
        return after_ref[part, pl.ds(rows, 16), pl.ds(lane + (f - history) * NCH, 128)]

    def store(device, tile):
        out_ref[pl.ds(device, 16), 0] = tile
        out_ref[pl.ds(device, 16), 1] = late_ref[pl.ds(device, 16)]

    filter_frames(read_own, taps_ref, x_ref.at[pl.ds(0, middle)])
    filter_frames(read_next, taps_ref, x_ref.at[pl.ds(middle, middle)])
    transform(x_ref, table_ref, wide_ref, store)


def order_kernel(recv_ref, real_ref, imag_ref):
    chans, tiles, halves, own, sub, _ = recv_ref.shape
    rows = chans * halves * sub // 2
    for channel in range(own):
        for pair in range(tiles // 2):

            def parts(tile):
                both = recv_ref[:, tile, :, channel].astype(jnp.float32)
                both = both.reshape(chans * halves, 2, sub // 2, 128)
                return [both[:, part].reshape(rows, 128).astype(jnp.bfloat16) for part in range(2)]

            first, second = parts(2 * pair), parts(2 * pair + 1)
            lanes = slice(pair * 128, pair * 128 + 128)
            for part, series_ref in enumerate((real_ref, imag_ref)):
                low = jnp.concatenate([first[part][:, :64], second[part][:, :64]], axis=1)
                high = jnp.concatenate([first[part][:, 64:], second[part][:, 64:]], axis=1)
                series_ref[channel, 0:rows, lanes] = low
                series_ref[channel, rows : 2 * rows, lanes] = high


def form_sums(series_refs, tiles, outs, channel, slot):
    inputs = series_refs[0].shape[1]
    samples = len(series_refs) * series_refs[0].shape[0] // 2
    rows = inputs // 16
    left = []
    for tile in tiles:
        lanes = pl.ds(pl.multiple_of(tile // 2 * 128, 128), 128)
        across = jnp.concatenate([ref[:, lanes].T for ref in series_refs], axis=1)
        left.append(jnp.where(tile % 2 == 0, across[:rows], across[rows:]))
    left = jnp.concatenate(left, axis=0)
    turned = jnp.concatenate([left[:, samples:], -left[:, :samples]], axis=1)
    both = jnp.concatenate([left, turned], axis=0)
    sums, start = 0.0, 0
    for ref in series_refs:
        depth = ref.shape[0]
        sums = sums + jnp.dot(both[:, start : start + depth], ref[...], preferred_element_type=jnp.float32)
        start += depth
    sums = sums * (1.0 / samples)
    count = left.shape[0]
    for n, out_ref in enumerate(outs):
        for part in range(2):
            start = part * count + n * rows
            out_ref[channel, slot, part] = sums[start : start + rows].astype(jnp.bfloat16)


def moved(position_ref, across, along):
    x, y, core = position_ref[0] // 4, position_ref[0] % 4, position_ref[1]
    dx, dy = jnp.where(core == 0, across, along), jnp.where(core == 0, along, across)
    return (x + dx) % 4 * 4 + (y + dy) % 4


def main_kernel(position_ref, *refs):
    series, outs = refs[:6], refs[6:]
    tiles = [moved(position_ref, shift, 0) for shift in SHIFTS]
    for channel in range(2):
        for slot in range(3):
            pieces = [ref.at[channel] for ref in series[2 * slot : 2 * slot + 2]]
            form_sums(pieces, tiles, outs, channel, slot)


def far_kernel(position_ref, *refs):
    series, outs = refs[:2], refs[2:]
    tiles = [moved(position_ref, shift, 0) for shift in SHIFTS]
    for channel in range(2):
        form_sums([ref.at[channel] for ref in series], tiles, outs, channel, 0)


def place_kernel(moves, position_ref, *refs):
    out_ref, out_sems = refs[-2:]
    copies = []
    for n, (shift, steps) in enumerate(moves):
        for channel in range(2):
            for slot, step in enumerate(steps):
                owner = moved(position_ref, 4 - shift, step)
                for part in range(2):
                    copy = pltpu.make_async_copy(
                        refs[n].at[channel, slot, part],
                        out_ref.at[part, owner * 2 + channel],
                        out_sems.at[len(copies)],
                    )
                    copy.start()
                    copies.append(copy)
    for copy in copies:
        copy.wait()


def gains_kernel(real_ref, imag_ref, flags_ref, out_ref):
    keep = (1 - flags_ref[...]).astype(jnp.float32)
    out_ref[...] = jnp.zeros_like(out_ref)
    for channel in range(2):
        for part, gain in enumerate(stefcal(real_ref.at[channel], imag_ref.at[channel], keep)):
            for tile in range(16):
                place = part * 2 + channel
                out_ref[tile, place : place + 1, 0:64] = gain[:, tile * 64 : tile * 64 + 64]


def stefcal(real_ref, imag_ref, keep):
    steps = real_ref.shape[0] // 16
    inverse = 1.0 / real_ref.shape[0]

    def load(step):
        start = pl.multiple_of(step * 16, 16)
        real = real_ref[pl.ds(start, 16), :].astype(jnp.float32)
        imag = imag_ref[pl.ds(start, 16), :].astype(jnp.float32)
        return real, imag

    def fold(value):
        return value[0:8] + value[8:16]

    zeros = jnp.zeros((8, keep.shape[1]), jnp.float32)

    def diagonal_step(step, carry):
        real, imag = load(step)
        return (
            carry[0] + fold(real * real + imag * imag),
            carry[1] + fold(imag * real - real * imag),
        )

    diag = lax.fori_loop(0, steps, diagonal_step, (zeros, zeros), unroll=4)
    diag_real = jnp.sum(diag[0], axis=0, keepdims=True) * inverse
    diag_imag = jnp.sum(diag[1], axis=0, keepdims=True) * inverse

    gain_real = keep
    gain_imag = jnp.zeros_like(keep)
    for iteration in range(ITERS):

        def times_step(step, carry, gain_real=gain_real, gain_imag=gain_imag):
            real, imag = load(step)
            mix_real = jnp.sum(real * gain_real + imag * gain_imag, axis=1, keepdims=True)
            mix_imag = jnp.sum(real * gain_imag - imag * gain_real, axis=1, keepdims=True)
            return (
                carry[0] + fold(real * mix_real - imag * mix_imag),
                carry[1] + fold(real * mix_imag + imag * mix_real),
            )

        sums = lax.fori_loop(0, steps, times_step, (zeros, zeros), unroll=4)
        num_real = jnp.sum(sums[0], axis=0, keepdims=True) * inverse
        num_imag = jnp.sum(sums[1], axis=0, keepdims=True) * inverse
        num_real = num_real - (diag_real * gain_real - diag_imag * gain_imag)
        num_imag = num_imag - (diag_real * gain_imag + diag_imag * gain_real)
        power = gain_real * gain_real + gain_imag * gain_imag
        denominator = jnp.sum(power, axis=1, keepdims=True) - power
        new_real = keep * num_real / denominator
        new_imag = keep * num_imag / denominator
        if iteration % 2 == 1:
            new_real = 0.5 * (new_real + gain_real)
            new_imag = 0.5 * (new_imag + gain_imag)
        gain_real, gain_imag = new_real, new_imag
    return gain_real, gain_imag


def params(mib=22):
    return pltpu.CompilerParams(vmem_limit_bytes=mib << 20)


def cost(flops, size):
    return pl.CostEstimate(flops=int(flops), bytes_accessed=int(size), transcendentals=0)


def turn(value, stage, shift):
    pairs = []
    for chan in range(lax.axis_size("chan")):
        for x in range(4):
            for y in range(4):
                to = (x, (y + shift) % 4) if chan % 2 == stage else ((x + shift) % 4, y)
                pairs.append((chan * 16 + x * 4 + y, chan * 16 + to[0] * 4 + to[1]))
    return lax.ppermute(value, ("chan", "tile"), pairs)


def place(position, parts, moves, out_shape, previous=None):
    operands = list(parts) + ([] if previous is None else [previous])
    anywhere = pl.BlockSpec(memory_space=pl.ANY)
    return pl.pallas_call(
        functools.partial(place_kernel, moves),
        in_specs=[pl.BlockSpec(memory_space=pltpu.SMEM)]
        + [pl.BlockSpec(memory_space=pltpu.VMEM)] * len(parts)
        + [anywhere] * (len(operands) - len(parts)),
        out_specs=anywhere,
        out_shape=out_shape,
        scratch_shapes=[pltpu.SemaphoreType.DMA((sum(4 * len(move[1]) for move in moves),))],
        input_output_aliases={} if previous is None else {len(operands): 0},
        compiler_params=params(10),
        cost_estimate=cost(0, len(parts) << 22),
        name="place",
    )(position, *operands)


def body(voltages, flags):
    row_count = voltages.shape[1]
    frame_count = voltages.shape[2] // NCH
    chan_count = lax.axis_size("chan")
    tile_count = lax.axis_size("tile")
    inputs = row_count * tile_count
    device_count = chan_count * tile_count
    own = NCH // device_count
    samples = frame_count * chan_count
    half = frame_count // 2
    sub = half

    taps = jnp.asarray(taps_table())
    table = jnp.asarray(dft_table(), jnp.bfloat16)
    scratch = [
        pltpu.VMEM((half * row_count, 2 * NCH), jnp.bfloat16),
        pltpu.VMEM((NCH * half, 128), jnp.float32),
    ]
    behind = TAPS - 1 - half // 2
    before = lax.ppermute(
        voltages[:, :, (frame_count - behind) * NCH :], "chan", [(c, c + 1) for c in range(chan_count - 1)]
    )
    after = lax.ppermute(
        voltages[:, :, : half // 2 * NCH], "chan", [(c, (c - 1) % chan_count) for c in range(chan_count)]
    )
    last = (lax.axis_index("chan") == chan_count - 1).astype(jnp.int32).reshape(1)
    late = pl.pallas_call(
        late_kernel,
        out_shape=jax.ShapeDtypeStruct((device_count, own, sub, 128), jnp.bfloat16),
        scratch_shapes=scratch,
        compiler_params=params(),
        cost_estimate=cost(1.5e9, 4 << 20),
        name="late_spectra",
    )(voltages, taps, table)
    spectra = pl.pallas_call(
        early_kernel,
        in_specs=[pl.BlockSpec(memory_space=pltpu.SMEM)] + [pl.BlockSpec(memory_space=pltpu.VMEM)] * 6,
        out_shape=jax.ShapeDtypeStruct((device_count, 2, own, sub, 128), jnp.bfloat16),
        scratch_shapes=scratch,
        compiler_params=params(),
        cost_estimate=cost(1.5e9, 6 << 20),
        name="early_spectra",
    )(last, voltages, before, after, late, taps, table)

    turned = lax.all_to_all(spectra, ("chan", "tile"), split_axis=0, concat_axis=0, tiled=True)
    turned = turned.reshape(chan_count, tile_count, 2, own, sub, 128)
    vmem = pl.BlockSpec(memory_space=pltpu.VMEM)
    smem = pl.BlockSpec(memory_space=pltpu.SMEM)
    series_shape = jax.ShapeDtypeStruct((own, samples, inputs), jnp.bfloat16)
    real, imag = pl.pallas_call(
        order_kernel,
        in_specs=[vmem],
        out_specs=[vmem] * 2,
        out_shape=[series_shape] * 2,
        compiler_params=params(),
        cost_estimate=cost(1e6, 4 << 20),
        name="order",
    )(turned)

    position = jnp.stack([lax.axis_index("tile"), lax.axis_index("chan") % 2]).astype(jnp.int32)
    up_real, down_imag = turn(real, 0, 1), turn(imag, 0, 3)
    up_imag, down_real = turn(imag, 0, 1), turn(real, 0, 3)
    far_real, far_imag = turn(up_real, 0, 1), turn(down_imag, 0, 3)
    gains = pl.pallas_call(
        gains_kernel,
        in_specs=[vmem] * 3,
        out_specs=vmem,
        out_shape=jax.ShapeDtypeStruct((tile_count, 8, 128), jnp.float32),
        compiler_params=params(12),
        cost_estimate=cost(own * inputs * samples * 64, 2 << 20),
        name="gains",
    )(real, imag, flags.reshape(1, inputs))
    up_imag, down_real, gains = lax.optimization_barrier((up_imag, down_real, gains))

    flops = 8 * 4 * row_count * inputs * samples
    blocks = pl.pallas_call(
        main_kernel,
        in_specs=[smem] + [vmem] * 6,
        out_specs=[vmem] * 4,
        out_shape=[jax.ShapeDtypeStruct((own, 3, 2, row_count, inputs), jnp.bfloat16)] * 4,
        compiler_params=params(),
        cost_estimate=cost(6 * flops, 12 << 20),
        name="main_sums",
    )(position, up_real, up_imag, down_real, down_imag, real, imag)
    blocks, far_real, far_imag = lax.optimization_barrier((blocks, far_real, far_imag))
    far_blocks = pl.pallas_call(
        far_kernel,
        in_specs=[smem] + [vmem] * 2,
        out_specs=[vmem] * 4,
        out_shape=[jax.ShapeDtypeStruct((own, 1, 2, row_count, inputs), jnp.bfloat16)] * 4,
        compiler_params=params(14),
        cost_estimate=cost(2 * flops, 4 << 20),
        name="far_sums",
    )(position, far_real, far_imag)

    near, far = (3, 1, 0), (2,)
    order = (1, 3, 2)
    sent = [turn(blocks[SHIFTS.index(shift)], 1, shift) for shift in order]
    sent_far = [turn(far_blocks[SHIFTS.index(shift)], 1, shift) for shift in order]
    out_shape = jax.ShapeDtypeStruct((2, tile_count * own, row_count, inputs), jnp.bfloat16)
    visibilities = place(position, [blocks[3], far_blocks[3]], [(0, near), (0, far)], out_shape)
    gains, sent[1], visibilities = lax.optimization_barrier((gains, sent[1], visibilities))
    gains = lax.all_to_all(gains, "tile", split_axis=0, concat_axis=0, tiled=True)
    moves = [(shift, steps) for steps in (near, far) for shift in order]
    visibilities = place(position, sent + sent_far, moves, out_shape, visibilities)
    gains = gains[:, : 2 * own, :row_count].reshape(tile_count, 2, own, row_count).transpose(1, 0, 2, 3)
    gains = gains.reshape(2, tile_count * own, row_count)
    return (visibilities, gains)


def solution(mesh):
    in_specs = (P(None, "tile", "chan"), P())
    out_specs = (P(None, "chan", "tile", None), P(None, "chan", "tile"))
    return jax.shard_map(body, mesh=mesh, in_specs=in_specs, out_specs=out_specs, check_vma=False)
```
